256 devices in a mesh: ctx: 16 (over y, x), tp: 16 (over z, core).
Axes of the slice: x: 4, y: 4, z: 8, core: 2. Of those that a mesh axis runs over, the one named last changes fastest.
Arguments:
- inner_act: bfloat16 [4096, 16384], P('ctx', 'tp'), may hold values from -6 to 6
- step_sizes: float32 [4096, 128], P('ctx', 'tp'), may hold values from 0.3 to 3
- in_coupling: bfloat16 [4096, 8, 128], P('ctx'), may hold values from -0.59765625 to 0.59765625
- out_coupling: bfloat16 [4096, 8, 128], P('ctx'), may hold values from -0.59765625 to 0.59765625
- log_rates: float32 [128], P('tp'), may hold values from -11.5 to -3.5
- skip_gain: float32 [128], P('tp'), may hold values from 0.5 to 2
- state_init: float32 [128, 128, 128], P('tp'), may hold values from -6 to 6
- out_weight: bfloat16 [16384, 8192], P('tp', 'ctx'), may hold values from -0.046875 to 0.046875
- cotangent: bfloat16 [4096, 8192], P('tp', 'ctx'), may hold values from -6 to 6
Outputs:
- mixed: bfloat16 [4096, 8192], P('tp', 'ctx')
- grad_inner: bfloat16 [4096, 16384], P('ctx', 'tp')
- grad_weight: bfloat16 [16384, 8192], P('tp', 'ctx')
- grad_state: float32 [128, 128, 128], P('tp', 'ctx')
The draws below stay inside these ranges and needn't reach their ends.
All inputs are finite; a program needn't handle non-finite values.
Results may differ from the reference program's by a relative error of at most 0.0049.
Values may be sent and summed in bfloat16 or wider, within the bound.
A program may use at most 128 MiB of HBM per device.

```python
import math
import jax
import jax.numpy as jnp
from jax import lax

D = 8192
H = 128
P_SIZE = 128
N = 128
G = 8
TOK_DEV = 256
TOKENS = 4096
E = 16384
N_CTX = 16


def block_scale(own_key, shape, cuts, low, top_value):
    def one(axis_at, blocks):
        heights = jax.random.uniform(jax.random.fold_in(jax.random.fold_in(own_key, 6), axis_at), (blocks,), jnp.float32, low / len(cuts), top_value / len(cuts))
        return jnp.repeat(jnp.exp(heights), shape[axis_at] // blocks).reshape((-1,) + (1,) * (len(shape) - axis_at - 1))

    loudness = one(*cuts[0])
    for cut in cuts[1:]:
        loudness = loudness * one(*cut)
    return loudness


def normal_values(stream_key, shape, deviation, bound, cuts=(), held_as=jnp.bfloat16):
    array = deviation * jax.random.normal(stream_key, shape, jnp.float32)
    if cuts:
        array = array * block_scale(stream_key, shape, cuts, -0.22, 0.18)
    return jnp.clip(array, -bound, bound).astype(held_as)


def setup_inputs(seed: int = 0) -> dict:
    arg_keys = jax.random.split(jax.random.key(seed), 10)
    return {
        "inner_act": normal_values(arg_keys[0], (TOKENS, E), 1.0, 6.0, ((0, 16), (1, 16))),
        "step_sizes": jnp.clip(jnp.exp(math.log(3.0) - 2.3025851 * jax.random.uniform(arg_keys[1], (TOKENS, H), jnp.float32) ** block_scale(arg_keys[1], (TOKENS, H), ((0, 16), (1, 16)), -0.2, 0.2)), 0.3, 3.0),
        "in_coupling": normal_values(arg_keys[2], (TOKENS, G, N), 0.09, 0.59765625, ((0, 16),)),
        "out_coupling": normal_values(arg_keys[3], (TOKENS, G, N), 0.09, 0.59765625, ((0, 16),)),
        "log_rates": jnp.clip(-11.5 + 8.0 * jax.random.uniform(arg_keys[4], (H,), jnp.float32) ** block_scale(arg_keys[4], (H,), ((0, 16),), -0.2, 0.2), -11.5, -3.5),
        "skip_gain": jnp.clip(0.5 + 1.5 * jax.random.uniform(arg_keys[5], (H,), jnp.float32) ** block_scale(arg_keys[5], (H,), ((0, 16),), -0.2, 0.2), 0.5, 2.0),
        "state_init": normal_values(arg_keys[6], (H, P_SIZE, N), 1.0, 6.0, ((0, 16),), jnp.float32),
        "out_weight": normal_values(arg_keys[7], (E, D), E ** -0.5, 0.046875, ((0, 16), (1, 16))),
        "cotangent": normal_values(arg_keys[8], (TOKENS, D), 1.0, 6.0, ((0, 16), (1, 16))),
    }


highest = lax.Precision.HIGHEST


def block_terms(step_block, write_block, read_block, rates):
    cumlog = jnp.cumsum(-step_block * rates[None, :], axis=0)
    length = cumlog.shape[0]
    causal = jnp.arange(length)[:, None] >= jnp.arange(length)[None, :]
    spread = cumlog.T[:, :, None] - cumlog.T[:, None, :]
    decays = jnp.where(causal[None], jnp.exp(jnp.where(causal[None], spread, 0.0)), 0.0)
    scores = jnp.einsum('thn,shn->hts', read_block, write_block, precision=highest) * decays
    trailing = jnp.exp(cumlog[-1][None, :] - cumlog)
    return cumlog, scores, trailing


def local_state(terms, values, step_block, write_block):
    cumlog, scores, trailing = terms
    inputs = step_block[:, :, None] * values
    own_state = jnp.einsum('sh,shp,shn->hpn', trailing, inputs, write_block, precision=highest)
    return jnp.exp(cumlog[-1]), own_state


def block_output(terms, values, step_block, read_block, skip_gain, state_in):
    cumlog, scores, trailing = terms
    inputs = step_block[:, :, None] * values
    inner = jnp.einsum('hts,shp->thp', scores, inputs, precision=highest)
    carried = jnp.exp(cumlog)[:, :, None] * jnp.einsum('thn,hpn->thp', read_block, state_in, precision=highest)
    return inner + carried + skip_gain[None, :, None] * values


def block_reach(terms, grad_block, read_block):
    cumlog, scores, trailing = terms
    return jnp.einsum('th,thp,thn->hpn', jnp.exp(cumlog), grad_block, read_block, precision=highest)


def block_grad_x(terms, grad_block, step_block, write_block, skip_gain, state_after):
    cumlog, scores, trailing = terms
    grad_in = jnp.einsum('hts,thp->shp', scores, grad_block, precision=highest)
    grad_in = grad_in + trailing[:, :, None] * jnp.einsum('hpn,shn->shp', state_after, write_block, precision=highest)
    return step_block[:, :, None] * grad_in + skip_gain[None, :, None] * grad_block


def reference(inner_act, step_sizes, in_coupling, out_coupling, log_rates, skip_gain, state_init, out_weight, cotangent):
    tokens = inner_act.shape[0]
    heads = step_sizes.shape[1]
    groups = in_coupling.shape[1]
    rates = jnp.exp(log_rates)
    values = inner_act.astype(jnp.float32).reshape(N_CTX, TOK_DEV, heads, P_SIZE)
    steps_all = step_sizes.reshape(N_CTX, TOK_DEV, heads)
    writes = jnp.repeat(in_coupling.astype(jnp.float32), heads // groups, axis=1).reshape(N_CTX, TOK_DEV, heads, N)
    reads = jnp.repeat(out_coupling.astype(jnp.float32), heads // groups, axis=1).reshape(N_CTX, TOK_DEV, heads, N)

    def forward_block(state_in, blocks):
        value_blk, step_blk, write_blk, read_blk = blocks
        terms = block_terms(step_blk, write_blk, read_blk, rates)
        block_decay, own_state = local_state(terms, value_blk, step_blk, write_blk)
        output = block_output(terms, value_blk, step_blk, read_blk, skip_gain, state_in)
        return block_decay[:, None, None] * state_in + own_state, output

    _, outputs = lax.scan(forward_block, state_init, (values, steps_all, writes, reads))
    mixer_out = outputs.reshape(tokens, heads * P_SIZE).astype(jnp.bfloat16)
    mixed = jnp.dot(mixer_out, out_weight, preferred_element_type=jnp.float32).astype(jnp.bfloat16)
    grad_mixer = lax.dot_general(cotangent, out_weight, (((1,), (1,)), ((), ())), preferred_element_type=jnp.float32)
    grad_weight = lax.dot_general(mixer_out, cotangent, (((0,), (0,)), ((), ())), preferred_element_type=jnp.float32).astype(jnp.bfloat16)
    grads = grad_mixer.reshape(N_CTX, TOK_DEV, heads, P_SIZE)

    def backward_block(state_after, blocks):
        grad_blk, step_blk, write_blk, read_blk = blocks
        terms = block_terms(step_blk, write_blk, read_blk, rates)
        reach = block_reach(terms, grad_blk, read_blk)
        grad_x = block_grad_x(terms, grad_blk, step_blk, write_blk, skip_gain, state_after)
        block_decay = jnp.exp(terms[0][-1])
        return reach + block_decay[:, None, None] * state_after, grad_x

    start_dual = jnp.zeros((heads, P_SIZE, N), jnp.float32)
    grad_state, grad_xs = lax.scan(backward_block, start_dual, (grads, steps_all, writes, reads), reverse=True)
    grad_inner = grad_xs.reshape(tokens, heads * P_SIZE).astype(jnp.bfloat16)
    return (mixed, grad_inner, grad_weight, grad_state)
```

```python
import jax
import jax.numpy as jnp
from jax import lax
from jax.experimental import pallas as pl
from jax.experimental.pallas import tpu as pltpu
from jax.sharding import PartitionSpec as P

f32 = jnp.float32
bf16 = jnp.bfloat16
L = 256
HD = 8
HH = HD // 2
S = 128
MODEL = 512
HALF = 512
NC = 16
NZ = 8


def mm(a, b):
    return lax.dot_general(a, b, (((1,), (0,)), ((), ())), preferred_element_type=f32)


def mm_bt(a, b):
    return lax.dot_general(a, b, (((1,), (1,)), ((), ())), preferred_element_type=f32)


def mm_at(a, b):
    return lax.dot_general(a, b, (((0,), (0,)), ((), ())), preferred_element_type=f32)


def split(v):
    hi = v.astype(bf16)
    return hi, (v - hi.astype(f32)).astype(bf16)


def rcopy(src, dst, send, recv, device):
    return pltpu.make_async_remote_copy(
        src_ref=src,
        dst_ref=dst,
        send_sem=send,
        recv_sem=recv,
        device_id=device,
        device_id_type=pl.DeviceIdType.MESH,
    )


def kernel(
    lograte_ref, skip_ref, step_ref, x_ref, b_ref, c_ref, init_ref, w_ref, cot_ref,
    mixed_ref, gi_ref, gw_ref, gs_ref,
    cot_all, pa, pb, r1a, r1b, r2a, r2b, r3a, r3b, r4a, r4b, ma, mb,
    own_mix, xs_mix, xr_mix, zs_mix, zr_mix, gw_acc, ybuf, gbuf,
    sb1, rb1, tb1, ub1, sb2, rb2, tb2, ub2,
    stp, cum_s, cumt_s, stept_s, bt_s, ct_s, cb_s,
    z_s, z_r, c_s, c_r, a1s, a1r, a2s, a2r, a3s, a3r, a4s, a4r,
    rsa_s, rsa_r, rsb_s, rsb_r, aga_s, aga_r, agb_s, agb_r, xm_s, xm_r, zm_s, zm_r,
):
    ctx = lax.axis_index("ctx")
    tp = lax.axis_index("tp")
    y, x = ctx // 4, ctx % 4
    z, k = tp // 2, tp % 2
    partner = z * 2 + (1 - k)

    def at_ctx(c):
        return (c, tp)

    def at_z(zz):
        return (ctx, zz * 2 + k)

    def at_y(yy):
        return (yy * 4 + x, tp)

    def at_x(xx):
        return (y * 4 + xx, tp)

    zp, zm = (z + 1) % NZ, (z + 7) % NZ
    other_core = (ctx, partner)

    def wait_in(dst, sem):
        rcopy(dst, dst, sem, sem, other_core).wait_recv()

    def wait_out(src, sem):
        rcopy(src, src, sem, sem, other_core).wait_send()

    barrier = pltpu.get_barrier_semaphore()

    @pl.loop(1, NC)
    def _(i):
        pl.semaphore_signal(
            barrier, inc=1, device_id=at_ctx((ctx + i) % NC), device_id_type=pl.DeviceIdType.MESH
        )

    @pl.loop(1, NZ)
    def _(i):
        pl.semaphore_signal(
            barrier, inc=1, device_id=at_z((z + i) % NZ), device_id_type=pl.DeviceIdType.MESH
        )

    pl.semaphore_signal(
        barrier, inc=1, device_id=other_core, device_id_type=pl.DeviceIdType.MESH
    )

    def zblock(d):
        return ((z + d + NZ) % NZ) * 2 + k

    def pblock(d):
        return ((z + d + NZ) % NZ) * 2 + (1 - k)

    top, bottom = pl.ds(0, L // 2), pl.ds(L // 2, L // 2)
    zcopies = []

    def zsend(src, dst, index, device):
        copy = rcopy(src, dst, z_s.at[index], z_r.at[index], device)
        copy.start()
        zcopies.append(copy)

    def csend(src, dst, index):
        copy = rcopy(src, dst, c_s.at[index], c_r.at[index], other_core)
        copy.start()
        zcopies.append(copy)

    def zstep(step):
        if step == 0:
            zsend(cot_ref, cot_all.at[tp], 0, at_z(zp))
            zsend(cot_ref, cot_all.at[tp], 1, at_z(zm))
            csend(cot_ref, cot_all.at[tp], 0)
            cot_all[tp] = cot_ref[...]
            return
        if step < 4:
            lo, hi = cot_all.at[zblock(-step)], cot_all.at[zblock(step)]
            wait_in(lo, z_r.at[2 * step - 2])
            if step < 3:
                zsend(lo, lo, 2 * step, at_z(zp))
            else:
                part = cot_all.at[zblock(-3), top]
                zsend(part, part, 6, at_z(zp))
            csend(lo, lo, 2 * step - 1)
            wait_in(hi, z_r.at[2 * step - 1])
            if step < 3:
                zsend(hi, hi, 2 * step + 1, at_z(zm))
            else:
                part = cot_all.at[zblock(3), bottom]
                zsend(part, part, 7, at_z(zm))
            csend(hi, hi, 2 * step)
            return
        wait_in(cot_all.at[zblock(4), top], z_r.at[6])
        wait_in(cot_all.at[zblock(4), bottom], z_r.at[7])
        whole = cot_all.at[zblock(4)]
        csend(whole, whole, 7)

    def zpartner(d):
        index = 0 if d == 0 else 7 if d == 4 else 2 * abs(d) - (1 if d < 0 else 0)
        wait_in(cot_all.at[pblock(d)], c_r.at[index])

    lane = lax.broadcasted_iota(jnp.int32, (L, S), 1)
    stp[...] = jnp.zeros_like(stp)
    stp[:, 0:HD] = step_ref[...]
    rate = jnp.exp(lograte_ref[...])
    row_i = lax.broadcasted_iota(jnp.int32, (L, L), 0)
    col_i = lax.broadcasted_iota(jnp.int32, (L, L), 1)
    tri = (row_i >= col_i).astype(f32)
    cum = lax.dot_general(
        tri, -stp[...] * rate, (((1,), (0,)), ((), ())),
        preferred_element_type=f32, precision=lax.Precision.HIGHEST,
    )
    cum_s[...] = cum
    cumt_s[...] = cum.T
    stept_s[...] = stp[...].T
    bt_s[...] = b_ref[...].astype(f32).T
    ct_s[...] = c_ref[...].astype(f32).T

    def col(ref, h):
        return jnp.sum(jnp.where(lane == h, ref[...], 0.0), axis=1, keepdims=True)

    def row(ref, h):
        return ref[pl.ds(h, 1), :]

    def heads(h):
        return pl.ds(pl.multiple_of(h * S, S), S)

    block_decay = jnp.broadcast_to(jnp.exp(cumt_s[0:HD, L - 1 : L]), (HD, S))

    def carry_send(p, sb, rb, ss, rs):
        @pl.loop(1, NC)
        def _(i):
            to = (ctx + i) % NC
            rcopy(
                sb.at[p, to], rb.at[p, ctx], ss.at[p * NC + to], rs.at[p * NC + ctx], at_ctx(to)
            ).start()

        rb[p, ctx] = sb[p, ctx]

    def carry_wait(p, ub, rs):
        @pl.loop(1, NC)
        def _(i):
            at = (ctx + i) % NC
            wait_in(ub.at[p, at], rs.at[p * NC + at])

    def carry_sent(sb, ss):
        for p in range(2):

            @pl.loop(1, NC)
            def _(i):
                to = (ctx + i) % NC
                wait_out(sb.at[p, to], ss.at[p * NC + to])

    def carry_scan(p, rb, tb, first, reverse):
        def hop(i, states):
            at = NC - 1 - i if reverse else i
            out = []
            for h in range(HH):
                tb[p, at, h] = states[h]
                out.append(rb[p, at, HH, h : h + 1, :] * states[h] + rb[p, at, h])
            return tuple(out)

        return lax.fori_loop(0, NC, hop, first)

    def put_piece(sb, p, h, state):
        sb[p, :, h] = state.reshape(NC, HD, S)

    def put_decay(sb, p):
        decay = block_decay[p * HH : (p + 1) * HH, :]
        sb[p, :, HH] = jnp.broadcast_to(jnp.concatenate([decay, decay])[None], (NC, HD, S))

    def own_states(p):
        @pl.loop(0, HH)
        def _(i):
            h = p * HH + i
            a_row = row(cumt_s, h)
            weight = jnp.exp(a_row[:, L - 1 : L] - a_row) * row(stept_s, h)
            hi, lo = split(bt_s[...] * weight)
            xh = x_ref[:, heads(h)]
            put_piece(sb1, p, i, (mm(hi, xh) + mm(lo, xh)).T)

        put_decay(sb1, p)

    def own_outputs(p):
        @pl.loop(p * HH, (p + 1) * HH)
        def _(h):
            a_col = col(cum_s, h)
            a_row = row(cumt_s, h)
            decay = jnp.where(row_i >= col_i, jnp.exp(jnp.minimum(a_col - a_row, 0.0)), 0.0)
            hi, lo = split(cb_s[...] * decay * row(stept_s, h))
            xh = x_ref[:, heads(h)]
            ybuf[:, heads(h)] = mm(hi, xh) + mm(lo, xh) + skip_ref[h] * xh.astype(f32)

    def scan_forward(p):
        carry_wait(p, rb1, a1r)
        first = tuple(
            init_ref[p * HH + i, pl.ds(pl.multiple_of(ctx * HD, HD), HD), :] for i in range(HH)
        )
        carry_scan(p, rb1, tb1, first, False)
        carry_send(p, tb1, ub1, a2s, a2r)

    def finish_outputs(p, m):
        carry_wait(p, ub1, a2r)

        @pl.loop(0, HH)
        def _(i):
            h = p * HH + i
            hi, lo = split(ub1[p, :, i].reshape(S, S))
            carried = jnp.exp(col(cum_s, h)) * (mm_bt(c_ref[...], hi) + mm_bt(c_ref[...], lo))
            m[ctx, :, heads(i)] = (ybuf[:, heads(h)] + carried).astype(bf16)

    own_states(0)
    pl.semaphore_wait(barrier, (NC - 1) + (NZ - 1) + 1)
    carry_send(0, sb1, rb1, a1s, a1r)
    zstep(0)
    own_states(1)
    carry_send(1, sb1, rb1, a1s, a1r)
    cb_s[...] = mm_bt(c_ref[...], b_ref[...])
    own_outputs(0)
    scan_forward(0)
    own_outputs(1)
    scan_forward(1)
    zstep(1)

    def partial_block(j):
        ct = cot_all[j]
        pa[j] = mm_bt(ct, w_ref[0:HALF, :]).astype(bf16)
        pb[j] = mm_bt(ct, w_ref[HALF : 2 * HALF, :]).astype(bf16)

    def partial_pair(d):
        zpartner(d)

        @pl.loop(0, 2)
        def _(i):
            partial_block(((z + d + NZ) % NZ) * 2 + i)

    def ring_sum(part, r1, r2, r3, r4, ss, rs, me1, me2, dev1, dev2, blk, gcol):
        n1p, n1m, far1 = (me1 + 1) % 4, (me1 + 3) % 4, (me1 + 2) % 4
        n2p, n2m = (me2 + 1) % 4, (me2 + 3) % 4
        copies = []

        def q(o):
            return (me2 + o) % 4

        def send(src, dst, index, device):
            copy = rcopy(src, dst, ss.at[index], rs.at[index], device)
            copy.start()
            copies.append(copy)

        plus, minus = (2, 1), (3, 0)

        def step1():
            for i in range(2):
                send(part.at[blk(far1, q(plus[i]))], r1.at[0, i], i, dev1(n1p))
                send(part.at[blk(far1, q(minus[i]))], r1.at[1, i], 2 + i, dev1(n1m))
            for o in minus:
                send(part.at[blk(n1p, q(o))], r2.at[0, o], 4 + o, dev1(n1p))
            for o in plus:
                send(part.at[blk(n1m, q(o))], r2.at[1, o], 8 + o, dev1(n1m))

        def step2():
            for i in range(2):
                for d, (near, order) in enumerate(((n1p, plus), (n1m, minus))):
                    o = order[i]
                    wait_in(r1.at[d, i], rs.at[2 * d + i])
                    j = blk(near, q(o))
                    part[j] = (part[j].astype(f32) + r1[d, i].astype(f32)).astype(bf16)
                    send(part.at[j], r2.at[d, o], 4 + 4 * d + o, dev1(near))

        def total(o):
            wait_in(r2.at[0, o], rs.at[4 + o])
            wait_in(r2.at[1, o], rs.at[8 + o])
            j = blk(me1, q(o))
            return part[j].astype(f32) + r2[0, o].astype(f32) + r2[1, o].astype(f32)

        def step3():
            j = blk(me1, q(2))
            part[j] = total(2).astype(bf16)
            send(part.at[j, top], r3.at[0], 12, dev2(n2p))
            send(part.at[j, bottom], r3.at[1], 13, dev2(n2m))

        def step4():
            for o, near, rows, d in ((1, n2p, top, 0), (3, n2m, bottom, 1)):
                j = blk(me1, q(o))
                part[j] = total(o).astype(bf16)
                wait_in(r3.at[d], rs.at[12 + d])
                part[j, rows] = (part[j, rows].astype(f32) + r3[d].astype(f32)).astype(bf16)
                send(part.at[j], r4.at[d], 14 + d, dev2(near))

        def step5():
            mine = total(0)
            wait_in(r4.at[0], rs.at[14])
            wait_in(r4.at[1], rs.at[15])
            gbuf[:, gcol : gcol + HALF] = mine + r4[0].astype(f32) + r4[1].astype(f32)

        return (step1, step2, step3, step4, step5), copies

    sum_a, copies_a = ring_sum(
        pa, r1a, r2a, r3a, r4a, rsa_s, rsa_r, y, x, at_y, at_x,
        lambda i1, i2: i1 * 4 + i2, 0,
    )
    sum_b, copies_b = ring_sum(
        pb, r1b, r2b, r3b, r4b, rsb_s, rsb_r, x, y, at_x, at_y,
        lambda i1, i2: i2 * 4 + i1, HALF,
    )

    def ring_gather(m, ss, rs, me1, me2, dev1, dev2, blk):
        n1p, n1m, far1 = (me1 + 1) % 4, (me1 + 3) % 4, (me1 + 2) % 4
        n2p, n2m, far2 = (me2 + 1) % 4, (me2 + 3) % 4, (me2 + 2) % 4
        copies = []

        def send(ref, index, device):
            copy = rcopy(ref, ref, ss.at[index], rs.at[index], device)
            copy.start()
            copies.append(copy)

        def at(o):
            return (me1 + o) % 4

        def across(o):
            ref = m.at[blk(at(o), me2)]
            send(ref, 4 + o, dev2(n2p))
            send(ref, 8 + o, dev2(n2m))

        def step1():
            ref = m.at[blk(me1, me2)]
            send(ref, 0, dev1(n1p))
            send(ref, 1, dev1(n1m))
            across(0)

        def step2():
            j = blk(n1m, me2)
            wait_in(m.at[j], rs.at[0])
            send(m.at[j, top], 2, dev1(n1p))
            j = blk(n1p, me2)
            wait_in(m.at[j], rs.at[1])
            send(m.at[j, bottom], 3, dev1(n1m))
            across(3)
            across(1)

        def step3():
            j = blk(far1, me2)
            wait_in(m.at[j, top], rs.at[2])
            wait_in(m.at[j, bottom], rs.at[3])
            across(2)

        def forward(o):
            lo, hi = m.at[blk(at(o), n2m)], m.at[blk(at(o), n2p)]
            wait_in(lo, rs.at[4 + o])
            wait_in(hi, rs.at[8 + o])
            if o in (0, 3):
                send(lo, 12 + o, dev2(n2p))
            else:
                send(hi, 12 + o, dev2(n2m))

        def last(o):
            wait_in(m.at[blk(at(o), far2)], rs.at[12 + o])

        return (step1, step2, step3, forward, last), copies

    gat_a, copies_ga = ring_gather(
        ma, aga_s, aga_r, x, y, at_x, at_y, lambda i1, i2: i2 * 4 + i1
    )
    gat_b, copies_gb = ring_gather(
        mb, agb_s, agb_r, y, x, at_y, at_x, lambda i1, i2: i1 * 4 + i2
    )

    def block_at(ry, rx):
        return ((y + ry) % 4) * 4 + (x + rx) % 4

    def project(j):
        return mm(ma[j], w_ref[0:HALF, :]) + mm(mb[j], w_ref[HALF : 2 * HALF, :])

    def pair(ry, low, high):
        turn = (x + low + k) % 2
        mine = low + turn * (high - low)
        return block_at(ry, mine), block_at(ry, low + high - mine)

    def pair_project(ry, low, high):
        mine, theirs = pair(ry, low, high)
        slot = theirs // 2
        xs_mix[slot] = project(theirs).astype(bf16)
        rcopy(xs_mix.at[slot], xr_mix.at[slot], xm_s.at[slot], xm_r.at[slot], other_core).start()
        own_mix[mine // 2] = project(mine).astype(bf16)

    def pair_send(ry, low, high):
        mine, _ = pair(ry, low, high)
        slot = mine // 2
        wait_in(xr_mix.at[slot], xm_r.at[slot])
        zs_mix[slot] = (own_mix[slot].astype(f32) + xr_mix[slot].astype(f32)).astype(bf16)

        @pl.when(slot != z)
        def _():
            rel = (z - slot + NZ) % NZ
            rcopy(
                zs_mix.at[slot], zr_mix.at[rel], zm_s.at[rel], zm_r.at[rel], (ctx, mine)
            ).start()

    gw_acc[...] = jnp.zeros_like(gw_acc)

    def weight_block(j):
        ct = cot_all[j]
        gw_acc[0:HALF, :] += mm_at(ma[j], ct)
        gw_acc[HALF : 2 * HALF, :] += mm_at(mb[j], ct)

    def pair_weight(ry, low, high):
        weight_block(block_at(ry, low))
        weight_block(block_at(ry, high))

    def own_reach(p):
        @pl.loop(0, HH)
        def _(i):
            h = p * HH + i
            ghi, glo = split(gbuf[:, heads(h)])
            hi, lo = split(ct_s[...] * jnp.exp(row(cumt_s, h)))
            put_piece(sb2, p, i, (mm(hi, ghi) + mm(lo, ghi) + mm(hi, glo)).T)

        put_decay(sb2, p)
        carry_send(p, sb2, rb2, a3s, a3r)

    def own_grads(p):
        @pl.loop(p * HH, (p + 1) * HH)
        def _(h):
            a_col = col(cum_s, h)
            a_row = row(cumt_s, h)
            decay = jnp.where(col_i >= row_i, jnp.exp(jnp.minimum(a_row - a_col, 0.0)), 0.0)
            hi, lo = split(cb_s[...] * decay)
            g = gbuf[:, heads(h)]
            ghi, glo = split(g)
            inner = mm(hi, ghi) + mm(lo, ghi) + mm(hi, glo)
            ybuf[:, heads(h)] = col(stp, h) * inner + skip_ref[h] * g

    def scan_backward(p):
        carry_wait(p, rb2, a3r)
        zero = jnp.zeros((HD, S), f32)
        done = carry_scan(p, rb2, tb2, (zero,) * HH, True)
        for i in range(HH):
            gs_ref[p * HH + i] = done[i]
        carry_send(p, tb2, ub2, a4s, a4r)

    def finish_grads(p):
        carry_wait(p, ub2, a4r)

        @pl.loop(0, HH)
        def _(i):
            h = p * HH + i
            hi, lo = split(ub2[p, :, i].reshape(S, S))
            a_col = col(cum_s, h)
            a_row = row(cumt_s, h)
            trailing = jnp.exp(a_row[:, L - 1 : L] - a_col)
            after = mm_bt(b_ref[...], hi) + mm_bt(b_ref[...], lo)
            total = ybuf[:, heads(h)] + col(stp, h) * trailing * after
            gi_ref[:, heads(h)] = total.astype(bf16)

    early = [(0, 0, 1), (1, 0, 1), (3, 0, 1)]
    late = [(0, 3, 2), (1, 3, 2), (3, 3, 2), (2, 0, 1), (2, 3, 2)]

    finish_outputs(0, ma)
    gat_a[0]()
    finish_outputs(1, mb)
    gat_b[0]()
    partial_pair(0)
    zstep(2)
    gat_a[1]()
    gat_b[1]()
    partial_pair(-1)
    partial_pair(1)
    zstep(3)
    gat_a[2]()
    gat_b[2]()
    partial_pair(-2)
    partial_pair(2)
    zstep(4)
    for o in (0, 3, 1):
        gat_a[3](o)
        gat_b[3](o)
    partial_pair(-3)
    partial_pair(3)
    partial_pair(4)
    gat_a[3](2)
    gat_b[3](2)
    sum_a[0]()
    sum_b[0]()
    for i, p in enumerate(early):
        pair_project(*p)
        if i:
            pair_send(*early[i - 1])
    pair_send(*early[-1])
    for o in (0, 3, 1, 2):
        gat_a[4](o)
        gat_b[4](o)
    for i, p in enumerate(late):
        pair_project(*p)
        if i:
            pair_send(*late[i - 1])
    pair_send(*late[-1])
    sum_a[1]()
    sum_b[1]()
    for p in early + late[:1]:
        pair_weight(*p)
    sum_a[2]()
    sum_b[2]()
    for p in late[1:]:
        pair_weight(*p)
    gw_ref[...] = gw_acc[...].astype(bf16)
    cb_s[...] = mm_bt(b_ref[...], c_ref[...])
    sum_a[3]()
    sum_b[3]()
    sum_a[4]()
    own_reach(0)
    sum_b[4]()
    own_reach(1)
    own_grads(0)
    scan_backward(0)
    own_grads(1)
    scan_backward(1)

    mixed = zs_mix[z].astype(f32)
    for rel in range(1, NZ):
        wait_in(zr_mix.at[rel], zm_r.at[rel])
        mixed = mixed + zr_mix[rel].astype(f32)
    mixed_ref[...] = mixed.astype(bf16)

    finish_grads(0)
    finish_grads(1)

    for copy in zcopies + copies_a + copies_b + copies_ga + copies_gb:
        copy.wait_send()
    carry_sent(sb1, a1s)
    carry_sent(tb1, a2s)
    carry_sent(sb2, a3s)
    carry_sent(tb2, a4s)

    @pl.loop(0, NZ)
    def _(i):
        wait_out(xs_mix.at[i], xm_s.at[i])

    @pl.loop(1, NZ)
    def _(i):
        wait_out(zr_mix.at[i], zm_s.at[i])


def local(inner_act, step_sizes, in_coupling, out_coupling, log_rates, skip_gain, state_init,
          out_weight, cotangent):
    group = lax.axis_index("tp") // 2
    write = lax.dynamic_index_in_dim(in_coupling, group, 1, keepdims=False)
    read = lax.dynamic_index_in_dim(out_coupling, group, 1, keepdims=False)
    rates = jnp.pad(log_rates.reshape(1, HD), ((0, 0), (0, S - HD)))
    vmem = pl.BlockSpec(memory_space=pltpu.VMEM)
    smem = pl.BlockSpec(memory_space=pltpu.SMEM)
    dma = pltpu.SemaphoreType.DMA
    V = pltpu.VMEM
    half = (L, HALF)
    mix = (L, MODEL)
    return pl.pallas_call(
        kernel,
        out_shape=(
            jax.ShapeDtypeStruct((L, MODEL), bf16),
            jax.ShapeDtypeStruct((L, HD * S), bf16),
            jax.ShapeDtypeStruct((HD * S, MODEL), bf16),
            jax.ShapeDtypeStruct((HD, HD, S), f32),
        ),
        in_specs=[vmem, smem] + [vmem] * 7,
        out_specs=(vmem,) * 4,
        scratch_shapes=[
            V((NC,) + mix, bf16),
            V((NC,) + half, bf16),
            V((NC,) + half, bf16),
            V((2, 2) + half, bf16),
            V((2, 2) + half, bf16),
            V((2, 4) + half, bf16),
            V((2, 4) + half, bf16),
            V((2, L // 2, HALF), bf16),
            V((2, L // 2, HALF), bf16),
            V((2,) + half, bf16),
            V((2,) + half, bf16),
            V((NC,) + half, bf16),
            V((NC,) + half, bf16),
            V((NZ,) + mix, bf16),
            V((NZ,) + mix, bf16),
            V((NZ,) + mix, bf16),
            V((NZ,) + mix, bf16),
            V((NZ,) + mix, bf16),
            V((2 * HALF, MODEL), f32),
            V((L, 2 * HALF), f32),
            V((L, 2 * HALF), f32),
            V((2, NC, HH + 1, HD, S), f32),
            V((2, NC, HH + 1, HD, S), f32),
            V((2, NC, HH, HD, S), f32),
            V((2, NC, HH, HD, S), f32),
            V((2, NC, HH + 1, HD, S), f32),
            V((2, NC, HH + 1, HD, S), f32),
            V((2, NC, HH, HD, S), f32),
            V((2, NC, HH, HD, S), f32),
            V((L, S), f32),
            V((L, S), f32),
            V((S, L), f32),
            V((S, L), f32),
            V((S, L), f32),
            V((S, L), f32),
            V((L, L), f32),
        ]
        + [dma((8,))] * 4
        + [dma((32,))] * 8
        + [dma((16,))] * 8
        + [dma((8,))] * 4,
        compiler_params=pltpu.CompilerParams(
            collective_id=0, has_side_effects=True, vmem_limit_bytes=62 * 1024 * 1024
        ),
        cost_estimate=pl.CostEstimate(
            flops=14_000_000_000, bytes_accessed=6_000_000, transcendentals=2_000_000
        ),
        name="mixer",
    )(rates, skip_gain, step_sizes, inner_act, write, read, state_init, out_weight, cotangent)


def solution(mesh):
    placed = (
        P("ctx", "tp"),
        P("ctx", "tp"),
        P("ctx", None, None),
        P("ctx", None, None),
        P("tp"),
        P("tp"),
        P("tp", None, None),
        P("tp", "ctx"),
        P("tp", "ctx"),
    )
    return jax.shard_map(
        local,
        mesh=mesh,
        in_specs=placed,
        out_specs=(P("tp", "ctx"), P("ctx", "tp"), P("tp", "ctx"), P("tp", "ctx", None)),
        check_vma=False,
    )
```

```python
import jax
import jax.numpy as jnp
from jax import lax
from jax.experimental import pallas as pl
from jax.experimental.pallas import tpu as pltpu
from jax.sharding import PartitionSpec as P

f32 = jnp.float32
bf16 = jnp.bfloat16
L = 256
HD = 8
HH = HD // 2
S = 128
MODEL = 512
HALF = 512
NC = 16
NZ = 8
NG = 8


def mm(a, b):
    return lax.dot_general(a, b, (((1,), (0,)), ((), ())), preferred_element_type=f32)


def mm_bt(a, b):
    return lax.dot_general(a, b, (((1,), (1,)), ((), ())), preferred_element_type=f32)


def mm_at(a, b):
    return lax.dot_general(a, b, (((0,), (0,)), ((), ())), preferred_element_type=f32)


def split(v):
    hi = v.astype(bf16)
    return hi, (v - hi.astype(f32)).astype(bf16)


def rcopy(src, dst, send, recv, device):
    return pltpu.make_async_remote_copy(
        src_ref=src,
        dst_ref=dst,
        send_sem=send,
        recv_sem=recv,
        device_id=device,
        device_id_type=pl.DeviceIdType.MESH,
    )


def kernel(
    lograte_ref, skip_ref, stept_ref, x_ref, in_ref, out_ref, init_ref, w_ref, cot_ref,
    mixed_ref, gi_ref, gw_ref, gs_ref,
    cot_all, pa, pb, r1a, r1b, r2a, r2b, r3a, r3b, r4a, r4b, ma, mb,
    own_mix, xs_mix, xr_mix, zs_mix, zr_mix, gw_acc, ybuf, gbuf,
    sb1, rb1, tb1, ub1, sb2, rb2, tb2, ub2,
    stp, cum_s, cumt_s, stept_s, bt_s, ct_s, cb_s, b_ref, c_ref,
    z_s, z_r, c_s, c_r, a1s, a1r, a2s, a2r, a3s, a3r, a4s, a4r,
    rsa_s, rsa_r, rsb_s, rsb_r, aga_s, aga_r, agb_s, agb_r, xm_s, xm_r, zm_s, zm_r,
):
    ctx = lax.axis_index("ctx")
    tp = lax.axis_index("tp")
    y, x = ctx // 4, ctx % 4
    z, k = tp // 2, tp % 2
    partner = z * 2 + (1 - k)

    def at_ctx(c):
        return (c, tp)

    def at_z(zz):
        return (ctx, zz * 2 + k)

    def at_y(yy):
        return (yy * 4 + x, tp)

    def at_x(xx):
        return (y * 4 + xx, tp)

    zp, zm = (z + 1) % NZ, (z + 7) % NZ
    other_core = (ctx, partner)

    def wait_in(dst, sem):
        rcopy(dst, dst, sem, sem, other_core).wait_recv()

    def wait_out(src, sem):
        rcopy(src, src, sem, sem, other_core).wait_send()

    barrier = pltpu.get_barrier_semaphore()

    @pl.loop(1, NC)
    def _(i):
        pl.semaphore_signal(
            barrier, inc=1, device_id=at_ctx((ctx + i) % NC), device_id_type=pl.DeviceIdType.MESH
        )

    @pl.loop(1, NZ)
    def _(i):
        pl.semaphore_signal(
            barrier, inc=1, device_id=at_z((z + i) % NZ), device_id_type=pl.DeviceIdType.MESH
        )

    pl.semaphore_signal(
        barrier, inc=1, device_id=other_core, device_id_type=pl.DeviceIdType.MESH
    )

    def zblock(d):
        return ((z + d + NZ) % NZ) * 2 + k

    def pblock(d):
        return ((z + d + NZ) % NZ) * 2 + (1 - k)

    top, bottom = pl.ds(0, L // 2), pl.ds(L // 2, L // 2)
    zcopies = []

    def zsend(src, dst, index, device):
        copy = rcopy(src, dst, z_s.at[index], z_r.at[index], device)
        copy.start()
        zcopies.append(copy)

    def csend(src, dst, index):
        copy = rcopy(src, dst, c_s.at[index], c_r.at[index], other_core)
        copy.start()
        zcopies.append(copy)

    def zstep(step):
        if step == 0:
            zsend(cot_ref, cot_all.at[tp], 0, at_z(zp))
            zsend(cot_ref, cot_all.at[tp], 1, at_z(zm))
            csend(cot_ref, cot_all.at[tp], 0)
            cot_all[tp] = cot_ref[...]
            return
        if step < 4:
            lo, hi = cot_all.at[zblock(-step)], cot_all.at[zblock(step)]
            wait_in(lo, z_r.at[2 * step - 2])
            if step < 3:
                zsend(lo, lo, 2 * step, at_z(zp))
            else:
                part = cot_all.at[zblock(-3), top]
                zsend(part, part, 6, at_z(zp))
            csend(lo, lo, 2 * step - 1)
            wait_in(hi, z_r.at[2 * step - 1])
            if step < 3:
                zsend(hi, hi, 2 * step + 1, at_z(zm))
            else:
                part = cot_all.at[zblock(3), bottom]
                zsend(part, part, 7, at_z(zm))
            csend(hi, hi, 2 * step)
            return
        wait_in(cot_all.at[zblock(4), top], z_r.at[6])
        wait_in(cot_all.at[zblock(4), bottom], z_r.at[7])
        whole = cot_all.at[zblock(4)]
        csend(whole, whole, 7)

    def zpartner(d):
        index = 0 if d == 0 else 7 if d == 4 else 2 * abs(d) - (1 if d < 0 else 0)
        wait_in(cot_all.at[pblock(d)], c_r.at[index])

    lane = lax.broadcasted_iota(jnp.int32, (L, S), 1)
    head_i = lax.broadcasted_iota(jnp.int32, (HD, L), 0)
    log_rate = jnp.zeros((HD, L), f32)
    for h in range(HD):
        log_rate = jnp.where(head_i == h, lograte_ref[h], log_rate)
    row_i = lax.broadcasted_iota(jnp.int32, (L, L), 0)
    col_i = lax.broadcasted_iota(jnp.int32, (L, L), 1)
    stept_s[...] = jnp.zeros_like(stept_s)
    stept_s[0:HD, :] = stept_ref[...]
    cumt_s[...] = jnp.zeros_like(cumt_s)
    cumt_s[0:HD, :] = lax.dot_general(
        -stept_ref[...] * jnp.exp(log_rate), (row_i <= col_i).astype(f32),
        (((1,), (0,)), ((), ())), preferred_element_type=f32, precision=lax.Precision.HIGHEST,
    )
    tok_i = lax.broadcasted_iota(jnp.int32, (L, NG * L), 0)
    tg_i = lax.broadcasted_iota(jnp.int32, (L, NG * L), 1)
    chosen = (tg_i == tok_i * NG + z).astype(bf16)
    b_ref[...] = mm(chosen, in_ref[...]).astype(bf16)
    bt_s[...] = b_ref[...].astype(f32).T

    def col(ref, h):
        return jnp.sum(jnp.where(lane == h, ref[...], 0.0), axis=1, keepdims=True)

    def row(ref, h):
        return ref[pl.ds(h, 1), :]

    def heads(h):
        return pl.ds(pl.multiple_of(h * S, S), S)

    block_decay = jnp.broadcast_to(jnp.exp(cumt_s[0:HD, L - 1 : L]), (HD, S))

    def carry_send(p, sb, rb, ss, rs):
        @pl.loop(1, NC)
        def _(i):
            to = (ctx + i) % NC
            rcopy(
                sb.at[p, to], rb.at[p, ctx], ss.at[p * NC + to], rs.at[p * NC + ctx], at_ctx(to)
            ).start()

        rb[p, ctx] = sb[p, ctx]

    def carry_wait(p, ub, rs):
        @pl.loop(1, NC)
        def _(i):
            at = (ctx + i) % NC
            wait_in(ub.at[p, at], rs.at[p * NC + at])

    def carry_sent(sb, ss):
        for p in range(2):

            @pl.loop(1, NC)
            def _(i):
                to = (ctx + i) % NC
                wait_out(sb.at[p, to], ss.at[p * NC + to])

    def carry_scan(p, rb, tb, first, reverse):
        def hop(i, states):
            at = NC - 1 - i if reverse else i
            out = []
            for h in range(HH):
                tb[p, at, h] = states[h]
                out.append(rb1[p, at, HH, h : h + 1, :] * states[h] + rb[p, at, h])
            return tuple(out)

        return lax.fori_loop(0, NC, hop, first)

    def put_piece(sb, p, h, state):
        sb[p, :, h] = state.reshape(NC, HD, S)

    def put_decay(sb, p):
        decay = block_decay[p * HH : (p + 1) * HH, :]
        sb[p, :, HH] = jnp.broadcast_to(jnp.concatenate([decay, decay])[None], (NC, HD, S))

    def own_states(p):
        @pl.loop(0, HH)
        def _(i):
            h = p * HH + i
            a_row = row(cumt_s, h)
            weight = jnp.exp(a_row[:, L - 1 : L] - a_row) * row(stept_s, h)
            hi, lo = split(bt_s[...] * weight)
            xh = x_ref[:, heads(h)]
            put_piece(sb1, p, i, (mm(hi, xh) + mm(lo, xh)).T)

        put_decay(sb1, p)

    def own_outputs(p):
        @pl.loop(p * HH, (p + 1) * HH)
        def _(h):
            a_col = col(cum_s, h)
            a_row = row(cumt_s, h)
            decay = jnp.where(row_i >= col_i, jnp.exp(jnp.minimum(a_col - a_row, 0.0)), 0.0)
            hi, lo = split(cb_s[...] * decay * row(stept_s, h))
            xh = x_ref[:, heads(h)]
            ybuf[:, heads(h)] = mm(hi, xh) + mm(lo, xh) + skip_ref[h] * xh.astype(f32)

    def scan_forward(p):
        carry_wait(p, rb1, a1r)
        first = tuple(
            init_ref[p * HH + i, pl.ds(pl.multiple_of(ctx * HD, HD), HD), :] for i in range(HH)
        )
        carry_scan(p, rb1, tb1, first, False)
        carry_send(p, tb1, ub1, a2s, a2r)

    def finish_outputs(p, m):
        carry_wait(p, ub1, a2r)

        @pl.loop(0, HH)
        def _(i):
            h = p * HH + i
            hi, lo = split(ub1[p, :, i].reshape(S, S))
            carried = jnp.exp(col(cum_s, h)) * (mm_bt(c_ref[...], hi) + mm_bt(c_ref[...], lo))
            m[ctx, :, heads(i)] = (ybuf[:, heads(h)] + carried).astype(bf16)

    own_states(0)
    pl.semaphore_wait(barrier, (NC - 1) + (NZ - 1) + 1)
    carry_send(0, sb1, rb1, a1s, a1r)
    zstep(0)
    own_states(1)
    carry_send(1, sb1, rb1, a1s, a1r)
    c_ref[...] = mm(chosen, out_ref[...]).astype(bf16)
    ct_s[...] = c_ref[...].astype(f32).T
    cum_s[...] = cumt_s[...].T
    stp[...] = stept_s[...].T
    cb_s[...] = mm_bt(c_ref[...], b_ref[...])
    scan_forward(0)
    own_outputs(0)
    scan_forward(1)
    zstep(1)

    def partial_block(j):
        ct = cot_all[j]
        pa[j] = mm_bt(ct, w_ref[0:HALF, :]).astype(bf16)
        pb[j] = mm_bt(ct, w_ref[HALF : 2 * HALF, :]).astype(bf16)

    def partial_pair(d):
        zpartner(d)

        @pl.loop(0, 2)
        def _(i):
            partial_block(((z + d + NZ) % NZ) * 2 + i)

    def ring_sum(part, r1, r2, r3, r4, ss, rs, me1, me2, dev1, dev2, blk, gcol):
        n1p, n1m, far1 = (me1 + 1) % 4, (me1 + 3) % 4, (me1 + 2) % 4
        n2p, n2m = (me2 + 1) % 4, (me2 + 3) % 4
        copies = []

        def q(o):
            return (me2 + o) % 4

        def send(src, dst, index, device):
            copy = rcopy(src, dst, ss.at[index], rs.at[index], device)
            copy.start()
            copies.append(copy)

        plus, minus = (2, 1), (3, 0)

        def step1():
            for i in range(2):
                send(part.at[blk(far1, q(plus[i]))], r1.at[0, i], i, dev1(n1p))
                send(part.at[blk(far1, q(minus[i]))], r1.at[1, i], 2 + i, dev1(n1m))
            send(part.at[blk(n1p, q(3))], r2.at[0, 3], 7, dev1(n1p))
            for o in plus:
                send(part.at[blk(n1m, q(o))], r2.at[1, o], 8 + o, dev1(n1m))

        def step2():
            for i in range(2):
                for d, (near, order) in enumerate(((n1p, plus), (n1m, minus))):
                    o = order[i]
                    wait_in(r1.at[d, i], rs.at[2 * d + i])
                    j = blk(near, q(o))
                    part[j] = (part[j].astype(f32) + r1[d, i].astype(f32)).astype(bf16)
                    send(part.at[j], r2.at[d, o], 4 + 4 * d + o, dev1(near))
            send(part.at[blk(n1p, q(0))], r2.at[0, 0], 4, dev1(n1p))

        def total(o):
            wait_in(r2.at[0, o], rs.at[4 + o])
            wait_in(r2.at[1, o], rs.at[8 + o])
            j = blk(me1, q(o))
            return part[j].astype(f32) + r2[0, o].astype(f32) + r2[1, o].astype(f32)

        def step3():
            j = blk(me1, q(2))
            part[j] = total(2).astype(bf16)
            send(part.at[j, top], r3.at[0], 12, dev2(n2p))
            send(part.at[j, bottom], r3.at[1], 13, dev2(n2m))

        def step4():
            for o, near, rows, d in ((3, n2m, bottom, 1), (1, n2p, top, 0)):
                j = blk(me1, q(o))
                part[j] = total(o).astype(bf16)
                wait_in(r3.at[d], rs.at[12 + d])
                part[j, rows] = (part[j, rows].astype(f32) + r3[d].astype(f32)).astype(bf16)
                send(part.at[j], r4.at[d], 14 + d, dev2(near))

        def step5():
            mine = total(0)
            wait_in(r4.at[0], rs.at[14])
            wait_in(r4.at[1], rs.at[15])
            gbuf[:, gcol : gcol + HALF] = mine + r4[0].astype(f32) + r4[1].astype(f32)

        return (step1, step2, step3, step4, step5), copies

    sum_a, copies_a = ring_sum(
        pa, r1a, r2a, r3a, r4a, rsa_s, rsa_r, y, x, at_y, at_x,
        lambda i1, i2: i1 * 4 + i2, 0,
    )
    sum_b, copies_b = ring_sum(
        pb, r1b, r2b, r3b, r4b, rsb_s, rsb_r, x, y, at_x, at_y,
        lambda i1, i2: i2 * 4 + i1, HALF,
    )

    def ring_gather(m, ss, rs, me1, me2, dev1, dev2, blk):
        n1p, n1m, far1 = (me1 + 1) % 4, (me1 + 3) % 4, (me1 + 2) % 4
        n2p, n2m, far2 = (me2 + 1) % 4, (me2 + 3) % 4, (me2 + 2) % 4
        copies = []

        def send(ref, index, device):
            copy = rcopy(ref, ref, ss.at[index], rs.at[index], device)
            copy.start()
            copies.append(copy)

        def at(o):
            return (me1 + o) % 4

        def across(o):
            ref = m.at[blk(at(o), me2)]
            send(ref, 4 + o, dev2(n2p))
            send(ref, 8 + o, dev2(n2m))

        def step1():
            ref = m.at[blk(me1, me2)]
            send(ref, 0, dev1(n1p))
            send(ref, 1, dev1(n1m))
            across(0)

        def step2():
            j = blk(n1m, me2)
            wait_in(m.at[j], rs.at[0])
            send(m.at[j, top], 2, dev1(n1p))
            j = blk(n1p, me2)
            wait_in(m.at[j], rs.at[1])
            send(m.at[j, bottom], 3, dev1(n1m))
            across(3)
            across(1)

        def step3():
            j = blk(far1, me2)
            wait_in(m.at[j, top], rs.at[2])
            wait_in(m.at[j, bottom], rs.at[3])
            across(2)

        def forward(o):
            lo, hi = m.at[blk(at(o), n2m)], m.at[blk(at(o), n2p)]
            wait_in(lo, rs.at[4 + o])
            wait_in(hi, rs.at[8 + o])
            if o in (0, 3):
                send(lo, 12 + o, dev2(n2p))
            else:
                send(hi, 12 + o, dev2(n2m))

        def last(o):
            wait_in(m.at[blk(at(o), far2)], rs.at[12 + o])

        return (step1, step2, step3, forward, last), copies

    gat_a, copies_ga = ring_gather(
        ma, aga_s, aga_r, x, y, at_x, at_y, lambda i1, i2: i2 * 4 + i1
    )
    gat_b, copies_gb = ring_gather(
        mb, agb_s, agb_r, y, x, at_y, at_x, lambda i1, i2: i1 * 4 + i2
    )

    def block_at(ry, rx):
        return ((y + ry) % 4) * 4 + (x + rx) % 4

    def project(j):
        return mm(ma[j], w_ref[0:HALF, :]) + mm(mb[j], w_ref[HALF : 2 * HALF, :])

    def pair(ry, low, high):
        turn = (x + low + k) % 2
        mine = low + turn * (high - low)
        return block_at(ry, mine), block_at(ry, low + high - mine)

    def pair_project(ry, low, high):
        mine, theirs = pair(ry, low, high)
        slot = theirs // 2
        xs_mix[slot] = project(theirs).astype(bf16)
        rcopy(xs_mix.at[slot], xr_mix.at[slot], xm_s.at[slot], xm_r.at[slot], other_core).start()
        own_mix[mine // 2] = project(mine).astype(bf16)

    def pair_send(ry, low, high):
        mine, _ = pair(ry, low, high)
        slot = mine // 2
        wait_in(xr_mix.at[slot], xm_r.at[slot])
        zs_mix[slot] = (own_mix[slot].astype(f32) + xr_mix[slot].astype(f32)).astype(bf16)

        @pl.when(slot != z)
        def _():
            rel = (z - slot + NZ) % NZ
            rcopy(
                zs_mix.at[slot], zr_mix.at[rel], zm_s.at[rel], zm_r.at[rel], (ctx, mine)
            ).start()

    gw_acc[...] = jnp.zeros_like(gw_acc)

    def weight_block(j):
        ct = cot_all[j]
        gw_acc[0:HALF, :] += mm_at(ma[j], ct)
        gw_acc[HALF : 2 * HALF, :] += mm_at(mb[j], ct)

    def pair_weight(ry, low, high):
        weight_block(block_at(ry, low))
        weight_block(block_at(ry, high))

    def own_reach(p):
        @pl.loop(0, HH)
        def _(i):
            h = p * HH + i
            ghi, glo = split(gbuf[:, heads(h)])
            hi, lo = split(ct_s[...] * jnp.exp(row(cumt_s, h)))
            put_piece(sb2, p, i, (mm(hi, ghi) + mm(lo, ghi) + mm(hi, glo)).T)

        carry_send(p, sb2, rb2, a3s, a3r)

    def own_grads(p):
        @pl.loop(p * HH, (p + 1) * HH)
        def _(h):
            a_col = col(cum_s, h)
            a_row = row(cumt_s, h)
            decay = jnp.where(col_i >= row_i, jnp.exp(jnp.minimum(a_row - a_col, 0.0)), 0.0)
            hi, lo = split(cb_s[...] * decay)
            g = gbuf[:, heads(h)]
            ghi, glo = split(g)
            inner = mm(hi, ghi) + mm(lo, ghi) + mm(hi, glo)
            ybuf[:, heads(h)] = col(stp, h) * inner + skip_ref[h] * g

    def scan_backward(p):
        carry_wait(p, rb2, a3r)
        zero = jnp.zeros((HD, S), f32)
        done = carry_scan(p, rb2, tb2, (zero,) * HH, True)
        for i in range(HH):
            gs_ref[p * HH + i] = done[i]
        carry_send(p, tb2, ub2, a4s, a4r)

    def finish_grads(p):
        carry_wait(p, ub2, a4r)

        @pl.loop(0, HH)
        def _(i):
            h = p * HH + i
            hi, lo = split(ub2[p, :, i].reshape(S, S))
            a_col = col(cum_s, h)
            a_row = row(cumt_s, h)
            trailing = jnp.exp(a_row[:, L - 1 : L] - a_col)
            after = mm_bt(b_ref[...], hi) + mm_bt(b_ref[...], lo)
            total = ybuf[:, heads(h)] + col(stp, h) * trailing * after
            gi_ref[:, heads(h)] = total.astype(bf16)

    early = [(0, 0, 1), (1, 0, 1), (3, 0, 1)]
    late = [(0, 3, 2), (1, 3, 2), (3, 3, 2), (2, 0, 1), (2, 3, 2)]

    finish_outputs(0, ma)
    gat_a[0]()
    own_outputs(1)
    finish_outputs(1, mb)
    gat_b[0]()
    partial_pair(0)
    zstep(2)
    gat_a[1]()
    gat_b[1]()
    partial_pair(-1)
    partial_pair(1)
    zstep(3)
    gat_a[2]()
    gat_b[2]()
    partial_pair(-2)
    partial_pair(2)
    zstep(4)
    for o in (0, 3, 1):
        gat_a[3](o)
        gat_b[3](o)
    partial_pair(-3)
    partial_pair(3)
    partial_pair(4)
    gat_a[3](2)
    gat_b[3](2)
    sum_a[0]()
    sum_b[0]()
    for i, p in enumerate(early):
        pair_project(*p)
        if i:
            pair_send(*early[i - 1])
    pair_send(*early[-1])
    for o in (0, 3, 1, 2):
        gat_a[4](o)
        gat_b[4](o)
    for i, p in enumerate(late):
        pair_project(*p)
        if i:
            pair_send(*late[i - 1])
    pair_send(*late[-1])
    sum_a[1]()
    sum_b[1]()
    for p in early + late:
        pair_weight(*p)
    sum_a[2]()
    sum_b[2]()
    sum_a[3]()
    sum_b[3]()
    gw_ref[...] = gw_acc[...].astype(bf16)
    cb_s[...] = mm_bt(b_ref[...], c_ref[...])
    sum_a[4]()
    own_reach(0)
    sum_b[4]()
    own_reach(1)
    own_grads(0)
    scan_backward(0)
    scan_backward(1)
    own_grads(1)

    mixed = zs_mix[z].astype(f32)
    for rel in range(1, NZ):
        wait_in(zr_mix.at[rel], zm_r.at[rel])
        mixed = mixed + zr_mix[rel].astype(f32)
    mixed_ref[...] = mixed.astype(bf16)

    finish_grads(0)
    finish_grads(1)

    for copy in zcopies + copies_a + copies_b + copies_ga + copies_gb:
        copy.wait_send()
    carry_sent(sb1, a1s)
    carry_sent(tb1, a2s)
    carry_sent(sb2, a3s)
    carry_sent(tb2, a4s)

    @pl.loop(0, NZ)
    def _(i):
        wait_out(xs_mix.at[i], xm_s.at[i])

    @pl.loop(1, NZ)
    def _(i):
        wait_out(zr_mix.at[i], zm_s.at[i])


def local(inner_act, step_sizes, in_coupling, out_coupling, log_rates, skip_gain, state_init,
          out_weight, cotangent):
    groups = in_coupling.shape[1]
    tokens = in_coupling.shape[0]
    vmem = pl.BlockSpec(memory_space=pltpu.VMEM)
    smem = pl.BlockSpec(memory_space=pltpu.SMEM)
    dma = pltpu.SemaphoreType.DMA
    V = pltpu.VMEM
    half = (L, HALF)
    mix = (L, MODEL)
    outs = pl.pallas_call(
        kernel,
        out_shape=(
            jax.ShapeDtypeStruct((L, MODEL), bf16),
            jax.ShapeDtypeStruct((L, HD * S), bf16),
            jax.ShapeDtypeStruct((HD * S, MODEL), bf16),
            jax.ShapeDtypeStruct((HD, HD, S), f32),
        ),
        in_specs=[smem, smem] + [vmem] * 7,
        out_specs=(vmem,) * 4,
        scratch_shapes=[
            V((NC,) + mix, bf16),
            V((NC,) + half, bf16),
            V((NC,) + half, bf16),
            V((2, 2) + half, bf16),
            V((2, 2) + half, bf16),
            V((2, 4) + half, bf16),
            V((2, 4) + half, bf16),
            V((2, L // 2, HALF), bf16),
            V((2, L // 2, HALF), bf16),
            V((2,) + half, bf16),
            V((2,) + half, bf16),
            V((NC,) + half, bf16),
            V((NC,) + half, bf16),
            V((NZ,) + mix, bf16),
            V((NZ,) + mix, bf16),
            V((NZ,) + mix, bf16),
            V((NZ,) + mix, bf16),
            V((NZ,) + mix, bf16),
            V((2 * HALF, MODEL), f32),
            V((L, 2 * HALF), f32),
            V((L, 2 * HALF), f32),
            V((2, NC, HH + 1, HD, S), f32),
            V((2, NC, HH + 1, HD, S), f32),
            V((2, NC, HH, HD, S), f32),
            V((2, NC, HH, HD, S), f32),
            V((2, NC, HH, HD, S), f32),
            V((2, NC, HH, HD, S), f32),
            V((2, NC, HH, HD, S), f32),
            V((2, NC, HH, HD, S), f32),
            V((L, S), f32),
            V((L, S), f32),
            V((S, L), f32),
            V((S, L), f32),
            V((S, L), f32),
            V((S, L), f32),
            V((L, L), f32),
            V((L, S), bf16),
            V((L, S), bf16),
        ]
        + [dma((8,))] * 4
        + [dma((32,))] * 8
        + [dma((16,))] * 8
        + [dma((8,))] * 4,
        compiler_params=pltpu.CompilerParams(
            collective_id=0, has_side_effects=True, vmem_limit_bytes=62 * 1024 * 1024
        ),
        cost_estimate=pl.CostEstimate(
            flops=14_000_000_000, bytes_accessed=6_000_000, transcendentals=2_000_000
        ),
        name="mixer",
    )(
        log_rates,
        skip_gain,
        step_sizes.T,
        inner_act,
        in_coupling.reshape(tokens * groups, S),
        out_coupling.reshape(tokens * groups, S),
        state_init,
        out_weight,
        cotangent,
    )

    hbm = pl.BlockSpec(memory_space=pl.ANY)
    return pl.pallas_call(
        hand_over,
        out_shape=tuple(jax.ShapeDtypeStruct(o.shape, o.dtype) for o in outs),
        in_specs=[hbm] * 4,
        out_specs=(hbm,) * 4,
        scratch_shapes=[V(o.shape, o.dtype) for o in outs] + [dma((4,))] * 2,
        name="hand_over",
    )(*outs)


def hand_over(*refs):
    held, into, out_of = refs[8:12], refs[12], refs[13]
    first = [pltpu.make_async_copy(refs[i], held[i], into.at[i]) for i in range(4)]
    last = [pltpu.make_async_copy(held[i], refs[4 + i], out_of.at[i]) for i in range(4)]
    for copy in first:
        copy.start()
    for i in range(4):
        first[i].wait()
        last[i].start()
    for copy in last:
        copy.wait()


def solution(mesh):
    placed = (
        P("ctx", "tp"),
        P("ctx", "tp"),
        P("ctx", None, None),
        P("ctx", None, None),
        P("tp"),
        P("tp"),
        P("tp", None, None),
        P("tp", "ctx"),
        P("tp", "ctx"),
    )
    return jax.shard_map(
        local,
        mesh=mesh,
        in_specs=placed,
        out_specs=(P("tp", "ctx"), P("ctx", "tp"), P("tp", "ctx"), P("tp", "ctx", None)),
        check_vma=False,
    )
```

```python
import jax
import jax.numpy as jnp
from jax import lax
from jax.experimental import pallas as pl
from jax.experimental.pallas import tpu as pltpu
from jax.sharding import PartitionSpec as P

f32 = jnp.float32
bf16 = jnp.bfloat16
L = 256
HD = 8
HH = HD // 2
S = 128
MODEL = 512
HALF = 512
NC = 16
NZ = 8
NG = 8


def mm(a, b):
    return lax.dot_general(a, b, (((1,), (0,)), ((), ())), preferred_element_type=f32)


def mm_bt(a, b):
    return lax.dot_general(a, b, (((1,), (1,)), ((), ())), preferred_element_type=f32)


def mm_at(a, b):
    return lax.dot_general(a, b, (((0,), (0,)), ((), ())), preferred_element_type=f32)


def split(v):
    hi = v.astype(bf16)
    return hi, (v - hi.astype(f32)).astype(bf16)


def rcopy(src, dst, send, recv, device):
    return pltpu.make_async_remote_copy(
        src_ref=src,
        dst_ref=dst,
        send_sem=send,
        recv_sem=recv,
        device_id=device,
        device_id_type=pl.DeviceIdType.MESH,
    )


def kernel(
    lograte_ref, skip_ref, stept_ref, x_ref, in_ref, out_ref, init_ref, w_ref, cot_ref,
    mixed_ref, gi_ref, gw_ref, gs_ref,
    cot_all, pa, pb, r1a, r1b, r2a, r2b, r3a, r3b, r4a, r4b, ma, mb,
    own_mix, xs_mix, xr_mix, zs_mix, zr_mix, gw_acc, ybuf, gbuf,
    sb1, rb1, tb1, ub1, sb2, rb2, tb2, ub2,
    stp, cum_s, cumt_s, stept_s, bt_s, ct_s, cb_s, b_ref, c_ref,
    z_s, z_r, c_s, c_r, a1s, a1r, a2s, a2r, a3s, a3r, a4s, a4r,
    rsa_s, rsa_r, rsb_s, rsb_r, aga_s, aga_r, agb_s, agb_r, xm_s, xm_r, zm_s, zm_r,
):
    ctx = lax.axis_index("ctx")
    tp = lax.axis_index("tp")
    y, x = ctx // 4, ctx % 4
    z, k = tp // 2, tp % 2
    partner = z * 2 + (1 - k)

    def at_ctx(c):
        return (c, tp)

    def at_z(zz):
        return (ctx, zz * 2 + k)

    def at_y(yy):
        return (yy * 4 + x, tp)

    def at_x(xx):
        return (y * 4 + xx, tp)

    zp, zm = (z + 1) % NZ, (z + 7) % NZ
    other_core = (ctx, partner)

    def wait_in(dst, sem):
        rcopy(dst, dst, sem, sem, other_core).wait_recv()

    def wait_out(src, sem):
        rcopy(src, src, sem, sem, other_core).wait_send()

    barrier = pltpu.get_barrier_semaphore()

    @pl.loop(1, NC)
    def _(i):
        pl.semaphore_signal(
            barrier, inc=1, device_id=at_ctx((ctx + i) % NC), device_id_type=pl.DeviceIdType.MESH
        )

    @pl.loop(1, NZ)
    def _(i):
        pl.semaphore_signal(
            barrier, inc=1, device_id=at_z((z + i) % NZ), device_id_type=pl.DeviceIdType.MESH
        )

    pl.semaphore_signal(
        barrier, inc=1, device_id=other_core, device_id_type=pl.DeviceIdType.MESH
    )

    def zblock(d):
        return ((z + d + NZ) % NZ) * 2 + k

    def pblock(d):
        return ((z + d + NZ) % NZ) * 2 + (1 - k)

    top, bottom = pl.ds(0, L // 2), pl.ds(L // 2, L // 2)
    zcopies = []

    def zsend(src, dst, index, device):
        copy = rcopy(src, dst, z_s.at[index], z_r.at[index], device)
        copy.start()
        zcopies.append(copy)

    def csend(src, dst, index):
        copy = rcopy(src, dst, c_s.at[index], c_r.at[index], other_core)
        copy.start()
        zcopies.append(copy)

    def zstep(step):
        if step == 0:
            zsend(cot_ref, cot_all.at[tp], 0, at_z(zp))
            zsend(cot_ref, cot_all.at[tp], 1, at_z(zm))
            csend(cot_ref, cot_all.at[tp], 0)
            cot_all[tp] = cot_ref[...]
            return
        if step < 4:
            lo, hi = cot_all.at[zblock(-step)], cot_all.at[zblock(step)]
            wait_in(lo, z_r.at[2 * step - 2])
            if step < 3:
                zsend(lo, lo, 2 * step, at_z(zp))
            else:
                part = cot_all.at[zblock(-3), top]
                zsend(part, part, 6, at_z(zp))
            csend(lo, lo, 2 * step - 1)
            wait_in(hi, z_r.at[2 * step - 1])
            if step < 3:
                zsend(hi, hi, 2 * step + 1, at_z(zm))
            else:
                part = cot_all.at[zblock(3), bottom]
                zsend(part, part, 7, at_z(zm))
            csend(hi, hi, 2 * step)
            return
        wait_in(cot_all.at[zblock(4), top], z_r.at[6])
        wait_in(cot_all.at[zblock(4), bottom], z_r.at[7])
        whole = cot_all.at[zblock(4)]
        csend(whole, whole, 7)

    def zpartner(d):
        index = 0 if d == 0 else 7 if d == 4 else 2 * abs(d) - (1 if d < 0 else 0)
        wait_in(cot_all.at[pblock(d)], c_r.at[index])

    lane = lax.broadcasted_iota(jnp.int32, (L, S), 1)
    head_i = lax.broadcasted_iota(jnp.int32, (HD, L), 0)
    log_rate = jnp.zeros((HD, L), f32)
    for h in range(HD):
        log_rate = jnp.where(head_i == h, lograte_ref[h], log_rate)
    row_i = lax.broadcasted_iota(jnp.int32, (L, L), 0)
    col_i = lax.broadcasted_iota(jnp.int32, (L, L), 1)
    stept_s[...] = jnp.zeros_like(stept_s)
    stept_s[0:HD, :] = stept_ref[...]
    cumt_s[...] = jnp.zeros_like(cumt_s)
    cumt_s[0:HD, :] = lax.dot_general(
        -stept_ref[...] * jnp.exp(log_rate), (row_i <= col_i).astype(f32),
        (((1,), (0,)), ((), ())), preferred_element_type=f32, precision=lax.Precision.HIGHEST,
    )
    tok_i = lax.broadcasted_iota(jnp.int32, (L, NG * L), 0)
    tg_i = lax.broadcasted_iota(jnp.int32, (L, NG * L), 1)
    chosen = (tg_i == tok_i * NG + z).astype(bf16)
    b_ref[...] = mm(chosen, in_ref[...]).astype(bf16)
    bt_s[...] = b_ref[...].astype(f32).T

    def col(ref, h):
        return jnp.sum(jnp.where(lane == h, ref[...], 0.0), axis=1, keepdims=True)

    def row(ref, h):
        return ref[pl.ds(h, 1), :]

    def heads(h):
        return pl.ds(pl.multiple_of(h * S, S), S)

    block_decay = jnp.broadcast_to(jnp.exp(cumt_s[0:HD, L - 1 : L]), (HD, S))

    def carry_send(p, sb, rb, ss, rs):
        @pl.loop(1, NC)
        def _(i):
            to = (ctx + i) % NC
            rcopy(
                sb.at[p, to], rb.at[p, ctx], ss.at[p * NC + to], rs.at[p * NC + ctx], at_ctx(to)
            ).start()

        rb[p, ctx] = sb[p, ctx]

    def carry_wait(p, ub, rs):
        @pl.loop(1, NC)
        def _(i):
            at = (ctx + i) % NC
            wait_in(ub.at[p, at], rs.at[p * NC + at])

    def carry_sent(sb, ss):
        for p in range(2):

            @pl.loop(1, NC)
            def _(i):
                to = (ctx + i) % NC
                wait_out(sb.at[p, to], ss.at[p * NC + to])

    def carry_scan(p, rb, tb, first, reverse):
        def hop(i, states):
            at = NC - 1 - i if reverse else i
            out = []
            for h in range(HH):
                tb[p, at, h] = states[h]
                out.append(rb1[p, at, HH, h : h + 1, :] * states[h] + rb[p, at, h])
            return tuple(out)

        return lax.fori_loop(0, NC, hop, first)

    def put_piece(sb, p, h, state):
        sb[p, :, h] = state.reshape(NC, HD, S)

    def put_decay(sb, p):
        decay = block_decay[p * HH : (p + 1) * HH, :]
        sb[p, :, HH] = jnp.broadcast_to(jnp.concatenate([decay, decay])[None], (NC, HD, S))

    def own_states(p):
        @pl.loop(0, HH)
        def _(i):
            h = p * HH + i
            a_row = row(cumt_s, h)
            weight = jnp.exp(a_row[:, L - 1 : L] - a_row) * row(stept_s, h)
            hi, lo = split(bt_s[...] * weight)
            xh = x_ref[:, heads(h)]
            put_piece(sb1, p, i, (mm(hi, xh) + mm(lo, xh)).T)

        put_decay(sb1, p)

    def own_outputs(p):
        @pl.loop(p * HH, (p + 1) * HH)
        def _(h):
            a_col = col(cum_s, h)
            a_row = row(cumt_s, h)
            decay = jnp.where(row_i >= col_i, jnp.exp(jnp.minimum(a_col - a_row, 0.0)), 0.0)
            hi, lo = split(cb_s[...] * decay * row(stept_s, h))
            xh = x_ref[:, heads(h)]
            ybuf[:, heads(h)] = mm(hi, xh) + mm(lo, xh) + skip_ref[h] * xh.astype(f32)

    def scan_forward(p):
        carry_wait(p, rb1, a1r)
        first = tuple(
            init_ref[p * HH + i, pl.ds(pl.multiple_of(ctx * HD, HD), HD), :] for i in range(HH)
        )
        carry_scan(p, rb1, tb1, first, False)
        carry_send(p, tb1, ub1, a2s, a2r)

    def finish_outputs(p, m):
        carry_wait(p, ub1, a2r)

        @pl.loop(0, HH)
        def _(i):
            h = p * HH + i
            hi, lo = split(ub1[p, :, i].reshape(S, S))
            carried = jnp.exp(col(cum_s, h)) * (mm_bt(c_ref[...], hi) + mm_bt(c_ref[...], lo))
            m[ctx, :, heads(i)] = (ybuf[:, heads(h)] + carried).astype(bf16)

    own_states(0)
    pl.semaphore_wait(barrier, (NC - 1) + (NZ - 1) + 1)
    carry_send(0, sb1, rb1, a1s, a1r)
    zstep(0)
    own_states(1)
    carry_send(1, sb1, rb1, a1s, a1r)
    c_ref[...] = mm(chosen, out_ref[...]).astype(bf16)
    ct_s[...] = c_ref[...].astype(f32).T
    cum_s[...] = cumt_s[...].T
    stp[...] = stept_s[...].T
    cb_s[...] = mm_bt(c_ref[...], b_ref[...])
    scan_forward(0)
    own_outputs(0)
    scan_forward(1)
    zstep(1)

    def partial_block(j):
        ct = cot_all[j]
        pa[j] = mm_bt(ct, w_ref[0:HALF, :]).astype(bf16)
        pb[j] = mm_bt(ct, w_ref[HALF : 2 * HALF, :]).astype(bf16)

    def partial_pair(d):
        zpartner(d)

        @pl.loop(0, 2)
        def _(i):
            partial_block(((z + d + NZ) % NZ) * 2 + i)

    def ring_sum(part, r1, r2, r3, r4, ss, rs, me1, me2, dev1, dev2, blk, gcol):
        n1p, n1m, far1 = (me1 + 1) % 4, (me1 + 3) % 4, (me1 + 2) % 4
        n2p, n2m = (me2 + 1) % 4, (me2 + 3) % 4
        copies = []

        def q(o):
            return (me2 + o) % 4

        def send(src, dst, index, device):
            copy = rcopy(src, dst, ss.at[index], rs.at[index], device)
            copy.start()
            copies.append(copy)

        plus, minus = (2, 1), (3, 0)

        def step1():
            for i in range(2):
                send(part.at[blk(far1, q(plus[i]))], r1.at[0, i], i, dev1(n1p))
                send(part.at[blk(far1, q(minus[i]))], r1.at[1, i], 2 + i, dev1(n1m))
            send(part.at[blk(n1p, q(3))], r2.at[0, 3], 7, dev1(n1p))
            for o in plus:
                send(part.at[blk(n1m, q(o))], r2.at[1, o], 8 + o, dev1(n1m))

        def step2():
            for i in range(2):
                for d, (near, order) in enumerate(((n1p, plus), (n1m, minus))):
                    o = order[i]
                    wait_in(r1.at[d, i], rs.at[2 * d + i])
                    j = blk(near, q(o))
                    part[j] = (part[j].astype(f32) + r1[d, i].astype(f32)).astype(bf16)
                    send(part.at[j], r2.at[d, o], 4 + 4 * d + o, dev1(near))
            send(part.at[blk(n1p, q(0))], r2.at[0, 0], 4, dev1(n1p))

        def total(o):
            wait_in(r2.at[0, o], rs.at[4 + o])
            wait_in(r2.at[1, o], rs.at[8 + o])
            j = blk(me1, q(o))
            return part[j].astype(f32) + r2[0, o].astype(f32) + r2[1, o].astype(f32)

        def step3():
            j = blk(me1, q(2))
            part[j] = total(2).astype(bf16)
            send(part.at[j, top], r3.at[0], 12, dev2(n2p))
            send(part.at[j, bottom], r3.at[1], 13, dev2(n2m))

        def step4():
            order = ((3, n2m, bottom, top, 1), (1, n2p, top, bottom, 0))
            for o, near, _, free, d in order:
                j = blk(me1, q(o))
                part[j] = total(o).astype(bf16)
                send(part.at[j, free], r4.at[d, free], 14 + d, dev2(near))
            for o, near, rows, _, d in order:
                j = blk(me1, q(o))
                wait_in(r3.at[d], rs.at[12 + d])
                part[j, rows] = (part[j, rows].astype(f32) + r3[d].astype(f32)).astype(bf16)
                send(part.at[j, rows], r4.at[d, rows], 16 + d, dev2(near))

        def step5():
            mine = total(0)
            for d, rows, free in ((0, top, bottom), (1, bottom, top)):
                wait_in(r4.at[d, free], rs.at[14 + d])
                wait_in(r4.at[d, rows], rs.at[16 + d])
            gbuf[:, gcol : gcol + HALF] = mine + r4[0].astype(f32) + r4[1].astype(f32)

        return (step1, step2, step3, step4, step5), copies

    sum_a, copies_a = ring_sum(
        pa, r1a, r2a, r3a, r4a, rsa_s, rsa_r, y, x, at_y, at_x,
        lambda i1, i2: i1 * 4 + i2, 0,
    )
    sum_b, copies_b = ring_sum(
        pb, r1b, r2b, r3b, r4b, rsb_s, rsb_r, x, y, at_x, at_y,
        lambda i1, i2: i2 * 4 + i1, HALF,
    )

    def ring_gather(m, ss, rs, me1, me2, dev1, dev2, blk):
        n1p, n1m, far1 = (me1 + 1) % 4, (me1 + 3) % 4, (me1 + 2) % 4
        n2p, n2m, far2 = (me2 + 1) % 4, (me2 + 3) % 4, (me2 + 2) % 4
        copies = []

        def send(ref, index, device):
            copy = rcopy(ref, ref, ss.at[index], rs.at[index], device)
            copy.start()
            copies.append(copy)

        def at(o):
            return (me1 + o) % 4

        def across(o):
            ref = m.at[blk(at(o), me2)]
            send(ref, 4 + o, dev2(n2p))
            send(ref, 8 + o, dev2(n2m))

        def step1():
            ref = m.at[blk(me1, me2)]
            send(ref, 0, dev1(n1p))
            send(ref, 1, dev1(n1m))
            across(0)

        def step2():
            j = blk(n1m, me2)
            wait_in(m.at[j], rs.at[0])
            send(m.at[j, top], 2, dev1(n1p))
            j = blk(n1p, me2)
            wait_in(m.at[j], rs.at[1])
            send(m.at[j, bottom], 3, dev1(n1m))
            across(3)
            across(1)

        def step3():
            j = blk(far1, me2)
            wait_in(m.at[j, top], rs.at[2])
            wait_in(m.at[j, bottom], rs.at[3])
            across(2)

        def forward(o):
            lo, hi = m.at[blk(at(o), n2m)], m.at[blk(at(o), n2p)]
            wait_in(lo, rs.at[4 + o])
            wait_in(hi, rs.at[8 + o])
            if o in (0, 3):
                send(lo, 12 + o, dev2(n2p))
            else:
                send(hi, 12 + o, dev2(n2m))

        def last(o):
            wait_in(m.at[blk(at(o), far2)], rs.at[12 + o])

        return (step1, step2, step3, forward, last), copies

    gat_a, copies_ga = ring_gather(
        ma, aga_s, aga_r, x, y, at_x, at_y, lambda i1, i2: i2 * 4 + i1
    )
    gat_b, copies_gb = ring_gather(
        mb, agb_s, agb_r, y, x, at_y, at_x, lambda i1, i2: i1 * 4 + i2
    )

    def block_at(ry, rx):
        return ((y + ry) % 4) * 4 + (x + rx) % 4

    def project(j):
        return mm(ma[j], w_ref[0:HALF, :]) + mm(mb[j], w_ref[HALF : 2 * HALF, :])

    def pair(ry, low, high):
        turn = (x + low + k) % 2
        mine = low + turn * (high - low)
        return block_at(ry, mine), block_at(ry, low + high - mine)

    def pair_project(ry, low, high):
        mine, theirs = pair(ry, low, high)
        slot = theirs // 2
        xs_mix[slot] = project(theirs).astype(bf16)
        rcopy(xs_mix.at[slot], xr_mix.at[slot], xm_s.at[slot], xm_r.at[slot], other_core).start()
        own_mix[mine // 2] = project(mine).astype(bf16)

    def pair_send(ry, low, high):
        mine, _ = pair(ry, low, high)
        slot = mine // 2
        wait_in(xr_mix.at[slot], xm_r.at[slot])
        zs_mix[slot] = (own_mix[slot].astype(f32) + xr_mix[slot].astype(f32)).astype(bf16)

        @pl.when(slot != z)
        def _():
            rel = (z - slot + NZ) % NZ
            rcopy(
                zs_mix.at[slot], zr_mix.at[rel], zm_s.at[rel], zm_r.at[rel], (ctx, mine)
            ).start()

    gw_acc[...] = jnp.zeros_like(gw_acc)

    def weight_block(j):
        ct = cot_all[j]
        gw_acc[0:HALF, :] += mm_at(ma[j], ct)
        gw_acc[HALF : 2 * HALF, :] += mm_at(mb[j], ct)

    def pair_weight(ry, low, high):
        weight_block(block_at(ry, low))
        weight_block(block_at(ry, high))

    def own_reach(p):
        @pl.loop(0, HH)
        def _(i):
            h = p * HH + i
            ghi, glo = split(gbuf[:, heads(h)])
            hi, lo = split(ct_s[...] * jnp.exp(row(cumt_s, h)))
            put_piece(sb2, p, i, (mm(hi, ghi) + mm(lo, ghi) + mm(hi, glo)).T)

        carry_send(p, sb2, rb2, a3s, a3r)

    def own_grads(p):
        @pl.loop(p * HH, (p + 1) * HH)
        def _(h):
            a_col = col(cum_s, h)
            a_row = row(cumt_s, h)
            decay = jnp.where(col_i >= row_i, jnp.exp(jnp.minimum(a_row - a_col, 0.0)), 0.0)
            hi, lo = split(cb_s[...] * decay)
            g = gbuf[:, heads(h)]
            ghi, glo = split(g)
            inner = mm(hi, ghi) + mm(lo, ghi) + mm(hi, glo)
            ybuf[:, heads(h)] = col(stp, h) * inner + skip_ref[h] * g

    def scan_backward(p):
        carry_wait(p, rb2, a3r)
        zero = jnp.zeros((HD, S), f32)
        done = carry_scan(p, rb2, tb2, (zero,) * HH, True)
        for i in range(HH):
            gs_ref[p * HH + i] = done[i]
        carry_send(p, tb2, ub2, a4s, a4r)

    def finish_grads(p):
        carry_wait(p, ub2, a4r)

        @pl.loop(0, HH)
        def _(i):
            h = p * HH + i
            hi, lo = split(ub2[p, :, i].reshape(S, S))
            a_col = col(cum_s, h)
            a_row = row(cumt_s, h)
            trailing = jnp.exp(a_row[:, L - 1 : L] - a_col)
            after = mm_bt(b_ref[...], hi) + mm_bt(b_ref[...], lo)
            total = ybuf[:, heads(h)] + col(stp, h) * trailing * after
            gi_ref[:, heads(h)] = total.astype(bf16)

    early = [(0, 0, 1), (1, 0, 1), (3, 0, 1)]
    late = [(0, 3, 2), (1, 3, 2), (3, 3, 2), (2, 0, 1), (2, 3, 2)]

    finish_outputs(0, ma)
    gat_a[0]()
    own_outputs(1)
    finish_outputs(1, mb)
    gat_b[0]()
    partial_pair(0)
    zstep(2)
    gat_a[1]()
    gat_b[1]()
    partial_pair(-1)
    partial_pair(1)
    zstep(3)
    gat_a[2]()
    gat_b[2]()
    partial_pair(-2)
    partial_pair(2)
    zstep(4)
    for o in (0, 3, 1):
        gat_a[3](o)
        gat_b[3](o)
    partial_pair(-3)
    partial_pair(3)
    partial_pair(4)
    gat_a[3](2)
    gat_b[3](2)
    sum_a[0]()
    sum_b[0]()
    for i, p in enumerate(early):
        pair_project(*p)
        if i:
            pair_send(*early[i - 1])
    pair_send(*early[-1])
    for o in (0, 3, 1, 2):
        gat_a[4](o)
        gat_b[4](o)
    for i, p in enumerate(late):
        pair_project(*p)
        if i:
            pair_send(*late[i - 1])
    pair_send(*late[-1])
    sum_a[1]()
    sum_b[1]()
    for p in early + late:
        pair_weight(*p)
    sum_a[2]()
    sum_b[2]()
    sum_a[3]()
    sum_b[3]()
    gw_ref[...] = gw_acc[...].astype(bf16)
    cb_s[...] = mm_bt(b_ref[...], c_ref[...])
    sum_a[4]()
    own_reach(0)
    sum_b[4]()
    own_reach(1)
    own_grads(0)
    scan_backward(0)
    scan_backward(1)
    own_grads(1)

    mixed = zs_mix[z].astype(f32)
    for rel in range(1, NZ):
        wait_in(zr_mix.at[rel], zm_r.at[rel])
        mixed = mixed + zr_mix[rel].astype(f32)
    mixed_ref[...] = mixed.astype(bf16)

    finish_grads(0)
    finish_grads(1)

    for copy in zcopies + copies_a + copies_b + copies_ga + copies_gb:
        copy.wait_send()
    carry_sent(sb1, a1s)
    carry_sent(tb1, a2s)
    carry_sent(sb2, a3s)
    carry_sent(tb2, a4s)

    @pl.loop(0, NZ)
    def _(i):
        wait_out(xs_mix.at[i], xm_s.at[i])

    @pl.loop(1, NZ)
    def _(i):
        wait_out(zr_mix.at[i], zm_s.at[i])


def local(inner_act, step_sizes, in_coupling, out_coupling, log_rates, skip_gain, state_init,
          out_weight, cotangent):
    groups = in_coupling.shape[1]
    tokens = in_coupling.shape[0]
    vmem = pl.BlockSpec(memory_space=pltpu.VMEM)
    smem = pl.BlockSpec(memory_space=pltpu.SMEM)
    dma = pltpu.SemaphoreType.DMA
    V = pltpu.VMEM
    half = (L, HALF)
    mix = (L, MODEL)
    outs = pl.pallas_call(
        kernel,
        out_shape=(
            jax.ShapeDtypeStruct((L, MODEL), bf16),
            jax.ShapeDtypeStruct((L, HD * S), bf16),
            jax.ShapeDtypeStruct((HD * S, MODEL), bf16),
            jax.ShapeDtypeStruct((HD, HD, S), f32),
        ),
        in_specs=[smem, smem] + [vmem] * 7,
        out_specs=(vmem,) * 4,
        scratch_shapes=[
            V((NC,) + mix, bf16),
            V((NC,) + half, bf16),
            V((NC,) + half, bf16),
            V((2, 2) + half, bf16),
            V((2, 2) + half, bf16),
            V((2, 4) + half, bf16),
            V((2, 4) + half, bf16),
            V((2, L // 2, HALF), bf16),
            V((2, L // 2, HALF), bf16),
            V((2,) + half, bf16),
            V((2,) + half, bf16),
            V((NC,) + half, bf16),
            V((NC,) + half, bf16),
            V((NZ,) + mix, bf16),
            V((NZ,) + mix, bf16),
            V((NZ,) + mix, bf16),
            V((NZ,) + mix, bf16),
            V((NZ,) + mix, bf16),
            V((2 * HALF, MODEL), f32),
            V((L, 2 * HALF), f32),
            V((L, 2 * HALF), f32),
            V((2, NC, HH + 1, HD, S), f32),
            V((2, NC, HH + 1, HD, S), f32),
            V((2, NC, HH, HD, S), f32),
            V((2, NC, HH, HD, S), f32),
            V((2, NC, HH, HD, S), f32),
            V((2, NC, HH, HD, S), f32),
            V((2, NC, HH, HD, S), f32),
            V((2, NC, HH, HD, S), f32),
            V((L, S), f32),
            V((L, S), f32),
            V((S, L), f32),
            V((S, L), f32),
            V((S, L), f32),
            V((S, L), f32),
            V((L, L), f32),
            V((L, S), bf16),
            V((L, S), bf16),
        ]
        + [dma((8,))] * 4
        + [dma((32,))] * 8
        + [dma((18,))] * 4
        + [dma((16,))] * 4
        + [dma((8,))] * 4,
        compiler_params=pltpu.CompilerParams(
            collective_id=0, has_side_effects=True, vmem_limit_bytes=62 * 1024 * 1024
        ),
        cost_estimate=pl.CostEstimate(
            flops=14_000_000_000, bytes_accessed=6_000_000, transcendentals=2_000_000
        ),
        name="mixer",
    )(
        log_rates,
        skip_gain,
        step_sizes.T,
        inner_act,
        in_coupling.reshape(tokens * groups, S),
        out_coupling.reshape(tokens * groups, S),
        state_init,
        out_weight,
        cotangent,
    )

    hbm = pl.BlockSpec(memory_space=pl.ANY)
    return pl.pallas_call(
        hand_over,
        out_shape=tuple(jax.ShapeDtypeStruct(o.shape, o.dtype) for o in outs),
        in_specs=[hbm] * 4,
        out_specs=(hbm,) * 4,
        scratch_shapes=[V(o.shape, o.dtype) for o in outs] + [dma((4,))] * 2,
        name="hand_over",
    )(*outs)


def hand_over(*refs):
    held, into, out_of = refs[8:12], refs[12], refs[13]
    first = [pltpu.make_async_copy(refs[i], held[i], into.at[i]) for i in range(4)]
    last = [pltpu.make_async_copy(held[i], refs[4 + i], out_of.at[i]) for i in range(4)]
    for copy in first:
        copy.start()
    for i in range(4):
        first[i].wait()
        last[i].start()
    for copy in last:
        copy.wait()


def solution(mesh):
    placed = (
        P("ctx", "tp"),
        P("ctx", "tp"),
        P("ctx", None, None),
        P("ctx", None, None),
        P("tp"),
        P("tp"),
        P("tp", None, None),
        P("tp", "ctx"),
        P("tp", "ctx"),
    )
    return jax.shard_map(
        local,
        mesh=mesh,
        in_specs=placed,
        out_specs=(P("tp", "ctx"), P("ctx", "tp"), P("tp", "ctx"), P("tp", "ctx", None)),
        check_vma=False,
    )
```

```python
import jax
import jax.numpy as jnp
from jax import lax
from jax.experimental import pallas as pl
from jax.experimental.pallas import tpu as pltpu
from jax.sharding import PartitionSpec as P

f32 = jnp.float32
bf16 = jnp.bfloat16
L = 256
HD = 8
HH = HD // 2
S = 128
MODEL = 512
HALF = 512
NC = 16
NZ = 8
NG = 8


def mm(a, b):
    return lax.dot_general(a, b, (((1,), (0,)), ((), ())), preferred_element_type=f32)


def mm_bt(a, b):
    return lax.dot_general(a, b, (((1,), (1,)), ((), ())), preferred_element_type=f32)


def mm_at(a, b):
    return lax.dot_general(a, b, (((0,), (0,)), ((), ())), preferred_element_type=f32)


def split(v):
    hi = v.astype(bf16)
    return hi, (v - hi.astype(f32)).astype(bf16)


def rcopy(src, dst, send, recv, device):
    return pltpu.make_async_remote_copy(
        src_ref=src,
        dst_ref=dst,
        send_sem=send,
        recv_sem=recv,
        device_id=device,
        device_id_type=pl.DeviceIdType.MESH,
    )


def kernel(
    lograte_ref, skip_ref, stept_ref, x_ref, in_ref, out_hbm, init_hbm, w_hbm, cot_ref,
    mixed_ref, gi_ref, gw_ref, gs_ref,
    cot_all, pa, pb, r1a, r1b, r2a, r2b, r3a, r3b, r4a, r4b, ma, mb,
    own_mix, xs_mix, xr_mix, zs_mix, zr_mix, gw_acc, ybuf, gbuf,
    sb1, rb1, tb1, ub1, sb2, rb2, tb2, ub2,
    stp, cum_s, cumt_s, stept_s, bt_s, ct_s, cb_s, b_ref, c_ref, gw_v, mixed_v, out_ref, init_ref, w_ref,
    z_s, z_r, c_s, c_r, a1s, a1r, a2s, a2r, a3s, a3r, a4s, a4r,
    rsa_s, rsa_r, rsb_s, rsb_r, aga_s, aga_r, agb_s, agb_r, xm_s, xm_r, zm_s, zm_r, out_sem, in_sem,
):
    ctx = lax.axis_index("ctx")
    tp = lax.axis_index("tp")
    y, x = ctx // 4, ctx % 4
    z, k = tp // 2, tp % 2
    partner = z * 2 + (1 - k)

    def at_ctx(c):
        return (c, tp)

    def at_z(zz):
        return (ctx, zz * 2 + k)

    def at_y(yy):
        return (yy * 4 + x, tp)

    def at_x(xx):
        return (y * 4 + xx, tp)

    zp, zm = (z + 1) % NZ, (z + 7) % NZ
    other_core = (ctx, partner)

    def wait_in(dst, sem):
        rcopy(dst, dst, sem, sem, other_core).wait_recv()

    def wait_out(src, sem):
        rcopy(src, src, sem, sem, other_core).wait_send()

    loads = [
        pltpu.make_async_copy(src, dst, in_sem.at[i])
        for i, (src, dst) in enumerate(((out_hbm, out_ref), (init_hbm, init_ref), (w_hbm, w_ref)))
    ]
    for load in loads:
        load.start()
    barrier = pltpu.get_barrier_semaphore()

    @pl.loop(1, NC)
    def _(i):
        pl.semaphore_signal(
            barrier, inc=1, device_id=at_ctx((ctx + i) % NC), device_id_type=pl.DeviceIdType.MESH
        )

    @pl.loop(1, NZ)
    def _(i):
        pl.semaphore_signal(
            barrier, inc=1, device_id=at_z((z + i) % NZ), device_id_type=pl.DeviceIdType.MESH
        )

    pl.semaphore_signal(
        barrier, inc=1, device_id=other_core, device_id_type=pl.DeviceIdType.MESH
    )

    def zblock(d):
        return ((z + d + NZ) % NZ) * 2 + k

    def pblock(d):
        return ((z + d + NZ) % NZ) * 2 + (1 - k)

    top, bottom = pl.ds(0, L // 2), pl.ds(L // 2, L // 2)
    zcopies = []

    def zsend(src, dst, index, device):
        copy = rcopy(src, dst, z_s.at[index], z_r.at[index], device)
        copy.start()
        zcopies.append(copy)

    def csend(src, dst, index):
        copy = rcopy(src, dst, c_s.at[index], c_r.at[index], other_core)
        copy.start()
        zcopies.append(copy)

    def zstep(step):
        if step == 0:
            zsend(cot_ref, cot_all.at[tp], 0, at_z(zp))
            zsend(cot_ref, cot_all.at[tp], 1, at_z(zm))
            csend(cot_ref, cot_all.at[tp], 0)
            cot_all[tp] = cot_ref[...]
            return
        if step < 4:
            lo, hi = cot_all.at[zblock(-step)], cot_all.at[zblock(step)]
            wait_in(lo, z_r.at[2 * step - 2])
            if step < 3:
                zsend(lo, lo, 2 * step, at_z(zp))
            else:
                part = cot_all.at[zblock(-3), top]
                zsend(part, part, 6, at_z(zp))
            csend(lo, lo, 2 * step - 1)
            wait_in(hi, z_r.at[2 * step - 1])
            if step < 3:
                zsend(hi, hi, 2 * step + 1, at_z(zm))
            else:
                part = cot_all.at[zblock(3), bottom]
                zsend(part, part, 7, at_z(zm))
            csend(hi, hi, 2 * step)
            return
        wait_in(cot_all.at[zblock(4), top], z_r.at[6])
        wait_in(cot_all.at[zblock(4), bottom], z_r.at[7])
        whole = cot_all.at[zblock(4)]
        csend(whole, whole, 7)

    def zpartner(d):
        index = 0 if d == 0 else 7 if d == 4 else 2 * abs(d) - (1 if d < 0 else 0)
        wait_in(cot_all.at[pblock(d)], c_r.at[index])

    lane = lax.broadcasted_iota(jnp.int32, (L, S), 1)
    head_i = lax.broadcasted_iota(jnp.int32, (HD, L), 0)
    log_rate = jnp.zeros((HD, L), f32)
    for h in range(HD):
        log_rate = jnp.where(head_i == h, lograte_ref[h], log_rate)
    row_i = lax.broadcasted_iota(jnp.int32, (L, L), 0)
    col_i = lax.broadcasted_iota(jnp.int32, (L, L), 1)
    stept_s[...] = jnp.zeros_like(stept_s)
    stept_s[0:HD, :] = stept_ref[...]
    cumt_s[...] = jnp.zeros_like(cumt_s)
    cumt_s[0:HD, :] = lax.dot_general(
        -stept_ref[...] * jnp.exp(log_rate), (row_i <= col_i).astype(f32),
        (((1,), (0,)), ((), ())), preferred_element_type=f32, precision=lax.Precision.HIGHEST,
    )
    tok_i = lax.broadcasted_iota(jnp.int32, (L, NG * L), 0)
    tg_i = lax.broadcasted_iota(jnp.int32, (L, NG * L), 1)
    chosen = (tg_i == tok_i * NG + z).astype(bf16)
    b_ref[...] = mm(chosen, in_ref[...]).astype(bf16)
    bt_s[...] = b_ref[...].astype(f32).T

    def col(ref, h):
        return jnp.sum(jnp.where(lane == h, ref[...], 0.0), axis=1, keepdims=True)

    def row(ref, h):
        return ref[pl.ds(h, 1), :]

    def heads(h):
        return pl.ds(pl.multiple_of(h * S, S), S)

    block_decay = jnp.broadcast_to(jnp.exp(cumt_s[0:HD, L - 1 : L]), (HD, S))

    def carry_send(p, sb, rb, ss, rs):
        @pl.loop(1, NC)
        def _(i):
            to = (ctx + i) % NC
            rcopy(
                sb.at[p, to], rb.at[p, ctx], ss.at[p * NC + to], rs.at[p * NC + ctx], at_ctx(to)
            ).start()

        rb[p, ctx] = sb[p, ctx]

    def carry_wait(p, ub, rs):
        @pl.loop(1, NC)
        def _(i):
            at = (ctx + i) % NC
            wait_in(ub.at[p, at], rs.at[p * NC + at])

    def carry_sent(sb, ss):
        for p in range(2):

            @pl.loop(1, NC)
            def _(i):
                to = (ctx + i) % NC
                wait_out(sb.at[p, to], ss.at[p * NC + to])

    def carry_scan(p, rb, tb, first, reverse):
        def hop(i, states):
            at = NC - 1 - i if reverse else i
            out = []
            for h in range(HH):
                tb[p, at, h] = states[h]
                out.append(rb1[p, at, HH, h : h + 1, :] * states[h] + rb[p, at, h])
            return tuple(out)

        return lax.fori_loop(0, NC, hop, first)

    def put_piece(sb, p, h, state):
        sb[p, :, h] = state.reshape(NC, HD, S)

    def put_decay(sb, p):
        decay = block_decay[p * HH : (p + 1) * HH, :]
        sb[p, :, HH] = jnp.broadcast_to(jnp.concatenate([decay, decay])[None], (NC, HD, S))

    def own_states(p):
        @pl.loop(0, HH)
        def _(i):
            h = p * HH + i
            a_row = row(cumt_s, h)
            weight = jnp.exp(a_row[:, L - 1 : L] - a_row) * row(stept_s, h)
            hi, lo = split(bt_s[...] * weight)
            xh = x_ref[:, heads(h)]
            put_piece(sb1, p, i, (mm(hi, xh) + mm(lo, xh)).T)

        put_decay(sb1, p)

    def own_outputs(p):
        @pl.loop(p * HH, (p + 1) * HH)
        def _(h):
            a_col = col(cum_s, h)
            a_row = row(cumt_s, h)
            decay = jnp.where(row_i >= col_i, jnp.exp(jnp.minimum(a_col - a_row, 0.0)), 0.0)
            hi, lo = split(cb_s[...] * decay * row(stept_s, h))
            xh = x_ref[:, heads(h)]
            ybuf[:, heads(h)] = mm(hi, xh) + mm(lo, xh) + skip_ref[h] * xh.astype(f32)

    def scan_forward(p):
        carry_wait(p, rb1, a1r)
        first = tuple(
            init_ref[p * HH + i, pl.ds(pl.multiple_of(ctx * HD, HD), HD), :] for i in range(HH)
        )
        carry_scan(p, rb1, tb1, first, False)
        carry_send(p, tb1, ub1, a2s, a2r)

    def finish_outputs(p, m):
        carry_wait(p, ub1, a2r)

        @pl.loop(0, HH)
        def _(i):
            h = p * HH + i
            hi, lo = split(ub1[p, :, i].reshape(S, S))
            carried = jnp.exp(col(cum_s, h)) * (mm_bt(c_ref[...], hi) + mm_bt(c_ref[...], lo))
            m[ctx, :, heads(i)] = (ybuf[:, heads(h)] + carried).astype(bf16)

    own_states(0)
    pl.semaphore_wait(barrier, (NC - 1) + (NZ - 1) + 1)
    carry_send(0, sb1, rb1, a1s, a1r)
    zstep(0)
    own_states(1)
    carry_send(1, sb1, rb1, a1s, a1r)
    for load in loads:
        load.wait()
    c_ref[...] = mm(chosen, out_ref[...]).astype(bf16)
    ct_s[...] = c_ref[...].astype(f32).T
    cum_s[...] = cumt_s[...].T
    stp[...] = stept_s[...].T
    cb_s[...] = mm_bt(c_ref[...], b_ref[...])
    scan_forward(0)
    own_outputs(0)
    scan_forward(1)
    zstep(1)

    def partial_block(j):
        ct = cot_all[j]
        pa[j] = mm_bt(ct, w_ref[0:HALF, :]).astype(bf16)
        pb[j] = mm_bt(ct, w_ref[HALF : 2 * HALF, :]).astype(bf16)

    def partial_pair(d):
        zpartner(d)

        @pl.loop(0, 2)
        def _(i):
            partial_block(((z + d + NZ) % NZ) * 2 + i)

    def ring_sum(part, r1, r2, r3, r4, ss, rs, me1, me2, dev1, dev2, blk, gcol):
        n1p, n1m, far1 = (me1 + 1) % 4, (me1 + 3) % 4, (me1 + 2) % 4
        n2p, n2m = (me2 + 1) % 4, (me2 + 3) % 4
        copies = []

        def q(o):
            return (me2 + o) % 4

        def send(src, dst, index, device):
            copy = rcopy(src, dst, ss.at[index], rs.at[index], device)
            copy.start()
            copies.append(copy)

        plus, minus = (2, 1), (3, 0)

        def step1():
            for i in range(2):
                send(part.at[blk(far1, q(plus[i]))], r1.at[0, i], i, dev1(n1p))
                send(part.at[blk(far1, q(minus[i]))], r1.at[1, i], 2 + i, dev1(n1m))
            send(part.at[blk(n1p, q(3))], r2.at[0, 3], 7, dev1(n1p))
            for o in plus:
                send(part.at[blk(n1m, q(o))], r2.at[1, o], 8 + o, dev1(n1m))

        def step2():
            for i in range(2):
                for d, (near, order) in enumerate(((n1p, plus), (n1m, minus))):
                    o = order[i]
                    wait_in(r1.at[d, i], rs.at[2 * d + i])
                    j = blk(near, q(o))
                    part[j] = (part[j].astype(f32) + r1[d, i].astype(f32)).astype(bf16)
                    send(part.at[j], r2.at[d, o], 4 + 4 * d + o, dev1(near))
            send(part.at[blk(n1p, q(0))], r2.at[0, 0], 4, dev1(n1p))

        def total(o):
            wait_in(r2.at[0, o], rs.at[4 + o])
            wait_in(r2.at[1, o], rs.at[8 + o])
            j = blk(me1, q(o))
            return part[j].astype(f32) + r2[0, o].astype(f32) + r2[1, o].astype(f32)

        def step3():
            j = blk(me1, q(2))
            part[j] = total(2).astype(bf16)
            send(part.at[j, top], r3.at[0], 12, dev2(n2p))
            send(part.at[j, bottom], r3.at[1], 13, dev2(n2m))

        def step4():
            for o, near, rows, d in ((3, n2m, bottom, 1), (1, n2p, top, 0)):
                j = blk(me1, q(o))
                part[j] = total(o).astype(bf16)
                wait_in(r3.at[d], rs.at[12 + d])
                part[j, rows] = (part[j, rows].astype(f32) + r3[d].astype(f32)).astype(bf16)
                send(part.at[j], r4.at[d], 14 + d, dev2(near))

        def step5():
            mine = total(0)
            wait_in(r4.at[0], rs.at[14])
            wait_in(r4.at[1], rs.at[15])
            gbuf[:, gcol : gcol + HALF] = mine + r4[0].astype(f32) + r4[1].astype(f32)

        return (step1, step2, step3, step4, step5), copies

    sum_a, copies_a = ring_sum(
        pa, r1a, r2a, r3a, r4a, rsa_s, rsa_r, y, x, at_y, at_x,
        lambda i1, i2: i1 * 4 + i2, 0,
    )
    sum_b, copies_b = ring_sum(
        pb, r1b, r2b, r3b, r4b, rsb_s, rsb_r, x, y, at_x, at_y,
        lambda i1, i2: i2 * 4 + i1, HALF,
    )

    def ring_gather(m, ss, rs, me1, me2, dev1, dev2, blk):
        n1p, n1m, far1 = (me1 + 1) % 4, (me1 + 3) % 4, (me1 + 2) % 4
        n2p, n2m, far2 = (me2 + 1) % 4, (me2 + 3) % 4, (me2 + 2) % 4
        copies = []

        def send(ref, index, device):
            copy = rcopy(ref, ref, ss.at[index], rs.at[index], device)
            copy.start()
            copies.append(copy)

        def at(o):
            return (me1 + o) % 4

        def across(o):
            ref = m.at[blk(at(o), me2)]
            send(ref, 4 + o, dev2(n2p))
            send(ref, 8 + o, dev2(n2m))

        def step1():
            ref = m.at[blk(me1, me2)]
            send(ref, 0, dev1(n1p))
            send(ref, 1, dev1(n1m))
            across(0)

        def step2():
            j = blk(n1m, me2)
            wait_in(m.at[j], rs.at[0])
            send(m.at[j, top], 2, dev1(n1p))
            j = blk(n1p, me2)
            wait_in(m.at[j], rs.at[1])
            send(m.at[j, bottom], 3, dev1(n1m))
            across(3)
            across(1)

        def step3():
            j = blk(far1, me2)
            wait_in(m.at[j, top], rs.at[2])
            wait_in(m.at[j, bottom], rs.at[3])
            across(2)

        def forward(o):
            lo, hi = m.at[blk(at(o), n2m)], m.at[blk(at(o), n2p)]
            wait_in(lo, rs.at[4 + o])
            wait_in(hi, rs.at[8 + o])
            if o in (0, 3):
                send(lo, 12 + o, dev2(n2p))
            else:
                send(hi, 12 + o, dev2(n2m))

        def last(o):
            wait_in(m.at[blk(at(o), far2)], rs.at[12 + o])

        return (step1, step2, step3, forward, last), copies

    gat_a, copies_ga = ring_gather(
        ma, aga_s, aga_r, x, y, at_x, at_y, lambda i1, i2: i2 * 4 + i1
    )
    gat_b, copies_gb = ring_gather(
        mb, agb_s, agb_r, y, x, at_y, at_x, lambda i1, i2: i1 * 4 + i2
    )

    def block_at(ry, rx):
        return ((y + ry) % 4) * 4 + (x + rx) % 4

    def project(j):
        return mm(ma[j], w_ref[0:HALF, :]) + mm(mb[j], w_ref[HALF : 2 * HALF, :])

    def pair(ry, low, high):
        turn = (x + low + k) % 2
        mine = low + turn * (high - low)
        return block_at(ry, mine), block_at(ry, low + high - mine)

    def pair_project(ry, low, high):
        mine, theirs = pair(ry, low, high)
        slot = theirs // 2
        xs_mix[slot] = project(theirs).astype(bf16)
        rcopy(xs_mix.at[slot], xr_mix.at[slot], xm_s.at[slot], xm_r.at[slot], other_core).start()
        own_mix[mine // 2] = project(mine).astype(bf16)

    def pair_send(ry, low, high):
        mine, _ = pair(ry, low, high)
        slot = mine // 2
        wait_in(xr_mix.at[slot], xm_r.at[slot])
        zs_mix[slot] = (own_mix[slot].astype(f32) + xr_mix[slot].astype(f32)).astype(bf16)

        @pl.when(slot != z)
        def _():
            rel = (z - slot + NZ) % NZ
            rcopy(
                zs_mix.at[slot], zr_mix.at[rel], zm_s.at[rel], zm_r.at[rel], (ctx, mine)
            ).start()

    gw_acc[...] = jnp.zeros_like(gw_acc)

    def weight_block(j):
        ct = cot_all[j]
        gw_acc[0:HALF, :] += mm_at(ma[j], ct)
        gw_acc[HALF : 2 * HALF, :] += mm_at(mb[j], ct)

    def pair_weight(ry, low, high):
        weight_block(block_at(ry, low))
        weight_block(block_at(ry, high))

    def own_reach(p):
        @pl.loop(0, HH)
        def _(i):
            h = p * HH + i
            ghi, glo = split(gbuf[:, heads(h)])
            hi, lo = split(ct_s[...] * jnp.exp(row(cumt_s, h)))
            put_piece(sb2, p, i, (mm(hi, ghi) + mm(lo, ghi) + mm(hi, glo)).T)

        carry_send(p, sb2, rb2, a3s, a3r)

    def own_grads(p):
        @pl.loop(p * HH, (p + 1) * HH)
        def _(h):
            a_col = col(cum_s, h)
            a_row = row(cumt_s, h)
            decay = jnp.where(col_i >= row_i, jnp.exp(jnp.minimum(a_row - a_col, 0.0)), 0.0)
            hi, lo = split(cb_s[...] * decay)
            g = gbuf[:, heads(h)]
            ghi, glo = split(g)
            inner = mm(hi, ghi) + mm(lo, ghi) + mm(hi, glo)
            ybuf[:, heads(h)] = col(stp, h) * inner + skip_ref[h] * g

    def scan_backward(p):
        carry_wait(p, rb2, a3r)
        zero = jnp.zeros((HD, S), f32)
        done = carry_scan(p, rb2, tb2, (zero,) * HH, True)
        for i in range(HH):
            gs_ref[p * HH + i] = done[i]
        carry_send(p, tb2, ub2, a4s, a4r)

    def finish_grads(p):
        carry_wait(p, ub2, a4r)

        @pl.loop(0, HH)
        def _(i):
            h = p * HH + i
            hi, lo = split(ub2[p, :, i].reshape(S, S))
            a_col = col(cum_s, h)
            a_row = row(cumt_s, h)
            trailing = jnp.exp(a_row[:, L - 1 : L] - a_col)
            after = mm_bt(b_ref[...], hi) + mm_bt(b_ref[...], lo)
            total = ybuf[:, heads(h)] + col(stp, h) * trailing * after
            gi_ref[:, heads(h)] = total.astype(bf16)

    early = [(0, 0, 1), (1, 0, 1), (3, 0, 1)]
    late = [(0, 3, 2), (1, 3, 2), (3, 3, 2), (2, 0, 1), (2, 3, 2)]

    finish_outputs(0, ma)
    gat_a[0]()
    own_outputs(1)
    finish_outputs(1, mb)
    gat_b[0]()
    partial_pair(0)
    zstep(2)
    gat_a[1]()
    gat_b[1]()
    partial_pair(-1)
    partial_pair(1)
    zstep(3)
    gat_a[2]()
    gat_b[2]()
    partial_pair(-2)
    partial_pair(2)
    zstep(4)
    for o in (0, 3, 1):
        gat_a[3](o)
        gat_b[3](o)
    partial_pair(-3)
    partial_pair(3)
    partial_pair(4)
    gat_a[3](2)
    gat_b[3](2)
    sum_a[0]()
    sum_b[0]()
    for i, p in enumerate(early):
        pair_project(*p)
        if i:
            pair_send(*early[i - 1])
    pair_send(*early[-1])
    for o in (0, 3, 1, 2):
        gat_a[4](o)
        gat_b[4](o)
    for i, p in enumerate(late):
        pair_project(*p)
        if i:
            pair_send(*late[i - 1])
    pair_send(*late[-1])
    sum_a[1]()
    sum_b[1]()
    for p in early + late:
        pair_weight(*p)
    sum_a[2]()
    sum_b[2]()
    sum_a[3]()
    sum_b[3]()
    gw_v[...] = gw_acc[...].astype(bf16)
    gw_out = pltpu.make_async_copy(gw_v, gw_ref, out_sem.at[0])
    gw_out.start()
    cb_s[...] = mm_bt(b_ref[...], c_ref[...])
    sum_a[4]()
    own_reach(0)
    sum_b[4]()
    own_reach(1)
    own_grads(0)
    scan_backward(0)
    scan_backward(1)
    own_grads(1)

    mixed = zs_mix[z].astype(f32)
    for rel in range(1, NZ):
        wait_in(zr_mix.at[rel], zm_r.at[rel])
        mixed = mixed + zr_mix[rel].astype(f32)
    mixed_v[...] = mixed.astype(bf16)
    mixed_out = pltpu.make_async_copy(mixed_v, mixed_ref, out_sem.at[1])
    mixed_out.start()

    finish_grads(0)
    finish_grads(1)

    gw_out.wait()
    mixed_out.wait()
    for copy in zcopies + copies_a + copies_b + copies_ga + copies_gb:
        copy.wait_send()
    carry_sent(sb1, a1s)
    carry_sent(tb1, a2s)
    carry_sent(sb2, a3s)
    carry_sent(tb2, a4s)

    @pl.loop(0, NZ)
    def _(i):
        wait_out(xs_mix.at[i], xm_s.at[i])

    @pl.loop(1, NZ)
    def _(i):
        wait_out(zr_mix.at[i], zm_s.at[i])


def local(inner_act, step_sizes, in_coupling, out_coupling, log_rates, skip_gain, state_init,
          out_weight, cotangent):
    groups = in_coupling.shape[1]
    tokens = in_coupling.shape[0]
    vmem = pl.BlockSpec(memory_space=pltpu.VMEM)
    smem = pl.BlockSpec(memory_space=pltpu.SMEM)
    dma = pltpu.SemaphoreType.DMA
    V = pltpu.VMEM
    half = (L, HALF)
    mix = (L, MODEL)
    outs = pl.pallas_call(
        kernel,
        out_shape=(
            jax.ShapeDtypeStruct((L, MODEL), bf16),
            jax.ShapeDtypeStruct((L, HD * S), bf16),
            jax.ShapeDtypeStruct((HD * S, MODEL), bf16),
            jax.ShapeDtypeStruct((HD, HD, S), f32),
        ),
        in_specs=[smem, smem] + [vmem] * 3 + [pl.BlockSpec(memory_space=pl.ANY)] * 3 + [vmem],
        out_specs=(pl.BlockSpec(memory_space=pl.ANY), vmem, pl.BlockSpec(memory_space=pl.ANY), vmem),
        scratch_shapes=[
            V((NC,) + mix, bf16),
            V((NC,) + half, bf16),
            V((NC,) + half, bf16),
            V((2, 2) + half, bf16),
            V((2, 2) + half, bf16),
            V((2, 4) + half, bf16),
            V((2, 4) + half, bf16),
            V((2, L // 2, HALF), bf16),
            V((2, L // 2, HALF), bf16),
            V((2,) + half, bf16),
            V((2,) + half, bf16),
            V((NC,) + half, bf16),
            V((NC,) + half, bf16),
            V((NZ,) + mix, bf16),
            V((NZ,) + mix, bf16),
            V((NZ,) + mix, bf16),
            V((NZ,) + mix, bf16),
            V((NZ,) + mix, bf16),
            V((2 * HALF, MODEL), f32),
            V((L, 2 * HALF), f32),
            V((L, 2 * HALF), f32),
            V((2, NC, HH + 1, HD, S), f32),
            V((2, NC, HH + 1, HD, S), f32),
            V((2, NC, HH, HD, S), f32),
            V((2, NC, HH, HD, S), f32),
            V((2, NC, HH, HD, S), f32),
            V((2, NC, HH, HD, S), f32),
            V((2, NC, HH, HD, S), f32),
            V((2, NC, HH, HD, S), f32),
            V((L, S), f32),
            V((L, S), f32),
            V((S, L), f32),
            V((S, L), f32),
            V((S, L), f32),
            V((S, L), f32),
            V((L, L), f32),
            V((L, S), bf16),
            V((L, S), bf16),
            V((HD * S, MODEL), bf16),
            V(mix, bf16),
            V((NG * L, S), bf16),
            V((HD, S, S), f32),
            V((HD * S, MODEL), bf16),
        ]
        + [dma((8,))] * 4
        + [dma((32,))] * 8
        + [dma((16,))] * 8
        + [dma((8,))] * 4
        + [dma((2,)), dma((3,))],
        compiler_params=pltpu.CompilerParams(
            collective_id=0, has_side_effects=True, vmem_limit_bytes=62 * 1024 * 1024
        ),
        cost_estimate=pl.CostEstimate(
            flops=14_000_000_000, bytes_accessed=6_000_000, transcendentals=2_000_000
        ),
        name="mixer",
    )(
        log_rates,
        skip_gain,
        step_sizes.T,
        inner_act,
        in_coupling.reshape(tokens * groups, S),
        out_coupling.reshape(tokens * groups, S),
        state_init,
        out_weight,
        cotangent,
    )

    hbm = pl.BlockSpec(memory_space=pl.ANY)
    return pl.pallas_call(
        hand_over,
        out_shape=tuple(jax.ShapeDtypeStruct(o.shape, o.dtype) for o in outs),
        in_specs=[hbm] * 4,
        out_specs=(hbm,) * 4,
        scratch_shapes=[V(o.shape, o.dtype) for o in outs] + [dma((4,))] * 2,
        name="hand_over",
    )(*outs)


def hand_over(*refs):
    held, into, out_of = refs[8:12], refs[12], refs[13]
    first = [pltpu.make_async_copy(refs[i], held[i], into.at[i]) for i in range(4)]
    last = [pltpu.make_async_copy(held[i], refs[4 + i], out_of.at[i]) for i in range(4)]
    for copy in first:
        copy.start()
    for i in range(4):
        first[i].wait()
        last[i].start()
    for copy in last:
        copy.wait()


def solution(mesh):
    placed = (
        P("ctx", "tp"),
        P("ctx", "tp"),
        P("ctx", None, None),
        P("ctx", None, None),
        P("tp"),
        P("tp"),
        P("tp", None, None),
        P("tp", "ctx"),
        P("tp", "ctx"),
    )
    return jax.shard_map(
        local,
        mesh=mesh,
        in_specs=placed,
        out_specs=(P("tp", "ctx"), P("ctx", "tp"), P("tp", "ctx"), P("tp", "ctx", None)),
        check_vma=False,
    )
```
